128 devices in a mesh: tm: 128 (over z, x, y, core).
Axes of the slice: x: 4, y: 4, z: 4, core: 2. Of those that a mesh axis runs over, the one named last changes fastest.
Arguments:
- transitions: float32 [1024, 256, 256], P('tm'), may hold values from -1 to 1
- noise_factor: float32 [1024, 256, 256], P('tm'), may hold values from -1 to 1, as said below
- forcing: float32 [1024, 256], P('tm'), may hold values from -0.3125 to 0.3125
- initial_mean: float32 [256], replicated, may hold values from -6 to 6
- initial_factor: float32 [256, 256], replicated, may hold values from -2 to 2, as said below
Outputs:
- means: float32 [1024, 256], P('tm')
- factors: float32 [1024, 256, 256], P('tm')
- log_scale: float32 [], replicated
The draws below stay inside these ranges and needn't reach their ends.
Inputs may be any that keep to these rules, and one draw needn't show every extreme that they name: `noise_factor`: each matrix is lower triangular with a positive diagonal. `initial_factor`: lower triangular with a positive diagonal.
All inputs are finite; a program needn't handle non-finite values.
Results may differ from the reference program's by a relative error of at most 0.0003.
Values sent between devices are 32-bit elements; how exact they have to be, the bound alone decides.
No kernel may reach another device: no remote copies, remote signals or barrier semaphores. Data moves between devices by JAX's collectives and lax.ppermute only.
A program may use at most 192 MiB of HBM per device.

```python
import math
import jax
import jax.numpy as jnp
from jax import lax

S = 256
HORIZON_LENGTH = 1024


spin = 0.02


def make_basis(key):
    key = jax.random.fold_in(key, 11)
    highest = lax.Precision.HIGHEST
    noise = jax.random.normal(key, (S, S), jnp.float32)
    matrix = (jnp.eye(S, dtype=jnp.float32) + 0.3 * noise / math.sqrt(S)) / 1.8
    for sweep in range(18):
        square = jnp.dot(matrix.T, matrix, precision=highest)
        matrix = 1.5 * matrix - 0.5 * jnp.dot(matrix, square, precision=highest)
    return matrix


def triangle(key, count, diag_scale, off_scale):
    keys = jax.random.split(key, 2)
    diag = jax.random.uniform(keys[0], (count, S), jnp.float32, 0.5, 1.0) * diag_scale
    off = jax.random.normal(keys[1], (count, S, S), jnp.float32) * off_scale / math.sqrt(S)
    lower = jnp.tril(off, -1)
    return lower + diag[:, :, None] * jnp.eye(S, dtype=jnp.float32)[None]


def draw_transitions(key, part):
    basis = make_basis(key)
    key = jax.random.fold_in(key, 1)
    keys = jax.random.split(key, 5)
    chain = float(HORIZON_LENGTH)
    tau = jnp.exp(jax.random.uniform(keys[0], (S,), jnp.float32, math.log(30.0), math.log(3.0 * chain)))
    rough = jax.random.uniform(keys[1], (HORIZON_LENGTH, S), jnp.float32, 0.5, 2.0)
    shrink_ratio = jnp.exp(-rough / tau[None, :])
    flagged_places = jax.random.randint(keys[2], (3,), 0, HORIZON_LENGTH)
    discarded_items = jax.random.uniform(keys[3], (3,), jnp.float32, 0.5, 0.8)
    epoch_locations = jnp.arange(HORIZON_LENGTH)
    clustered_runs = jnp.ones((HORIZON_LENGTH,), jnp.float32)
    for chosen_location in range(3):
        clustered_runs = jnp.where(epoch_locations == flagged_places[chosen_location], clustered_runs * discarded_items[chosen_location], clustered_runs)
    shrink_ratio = shrink_ratio * clustered_runs[:, None]
    symmetric = jnp.einsum('ij,tj,kj->tik', basis, shrink_ratio, basis, precision=lax.Precision.HIGHEST)
    twist = jax.random.normal(keys[4], (HORIZON_LENGTH, S, S), jnp.float32)
    skew = (twist - jnp.swapaxes(twist, 1, 2)) * (spin / math.sqrt(2.0 * S))
    return (symmetric + skew) * math.exp(-spin * spin)


def draw_noise_factor(key, part):
    key = jax.random.fold_in(key, 2)
    keys = jax.random.split(key, 1)
    result = triangle(keys[0], HORIZON_LENGTH, 0.03, 0.015)
    return result


def draw_initial_factor(key, part):
    key = jax.random.fold_in(key, 3)
    keys = jax.random.split(key, 1)
    result = triangle(keys[0], 1, 1.0, 0.5)[0]
    return result


def shard_levels(rng, shape, pieces, low, high):
    def one(dim, shards_of):
        draws = jax.random.uniform(jax.random.fold_in(jax.random.fold_in(rng, 6), dim), (shards_of,), jnp.float32, low / len(pieces), high / len(pieces))
        return jnp.repeat(jnp.exp(draws), shape[dim] // shards_of).reshape((-1,) + (1,) * (len(shape) - dim - 1))

    level = one(*pieces[0])
    for cut in pieces[1:]:
        level = level * one(*cut)
    return level


def gaussian(own_key, extent, width, bound, pieces=(), kind=jnp.bfloat16):
    values = jax.random.normal(own_key, extent, jnp.float32) * width
    if len(pieces) > 0:
        values = shard_levels(own_key, extent, pieces, -0.22, 0.18) * values
    return jnp.clip(values, min=-bound, max=bound).astype(kind)


def setup_inputs(seed: int = 0) -> dict:
    arg_keys = jax.random.split(jax.random.key(seed), 6)
    transitions = draw_transitions(jax.random.fold_in(arg_keys[5], 71), 0)
    noise_factor = draw_noise_factor(jax.random.fold_in(arg_keys[5], 71), 0)
    forcing = gaussian(arg_keys[2], (HORIZON_LENGTH, S), 0.05, 0.3125, ((0, 128),), jnp.float32)
    initial_mean = gaussian(arg_keys[3], (S,), 1.0, 6.0, (), jnp.float32)
    initial_factor = draw_initial_factor(jax.random.fold_in(arg_keys[5], 71), 0)
    return dict(transitions=transitions, noise_factor=noise_factor, forcing=forcing, initial_mean=initial_mean, initial_factor=initial_factor)


def reference(transitions, noise_factor, forcing, initial_mean, initial_factor):
    highest = lax.Precision.HIGHEST
    start_cov = jnp.dot(initial_factor, initial_factor.T, precision=highest)

    def advance(carry, step):
        mean, cov = carry
        trans, factor, push = step
        mean = jnp.dot(trans, mean, precision=highest) + push
        noise = jnp.dot(factor, factor.T, precision=highest)
        cov = jnp.dot(jnp.dot(trans, cov, precision=highest), trans.T, precision=highest) + noise
        return ((mean, cov), (mean, jnp.linalg.cholesky(cov)))
    final_state, stacked = lax.scan(advance, (initial_mean, start_cov), (transitions, noise_factor, forcing))
    means, factors = stacked
    log_scale = jnp.mean(jnp.log(jnp.diagonal(factors, axis1=1, axis2=2)))
    return (means, factors, log_scale)
```

```python
import jax
import jax.numpy as jnp
from jax import lax
from jax.experimental import pallas as pl
from jax.experimental.pallas import tpu as pltpu
from jax.sharding import Mesh, PartitionSpec as P

f32, bf16 = jnp.float32, jnp.bfloat16
AXES = ("z", "x", "y", "c")
N = 256
H = 128
STEPS = 8
ROWS = 400
HALF = ROWS // 2
PB = 8


def split(x):
    hi = x.astype(bf16)
    return hi, (x - hi.astype(f32)).astype(bf16)


def dg(a, b, ca, cb):
    return lax.dot_general(a, b, (((ca,), (cb,)), ((), ())), preferred_element_type=f32)


def mm3(a, b, ca=1, cb=0):
    return dg(a[0], b[0], ca, cb) + (dg(a[0], b[1], ca, cb) + dg(a[1], b[0], ca, cb))


def row_times(vec, a):
    v1 = vec.astype(bf16)
    rest = vec - v1.astype(f32)
    v2 = rest.astype(bf16)
    v3 = (rest - v2.astype(f32)).astype(bf16)
    out = dg(v3, a[0], 1, 1) + dg(v2, a[1], 1, 1)
    out = out + (dg(v2, a[0], 1, 1) + dg(v1, a[1], 1, 1))
    return out + dg(v1, a[0], 1, 1)


def grid_iota():
    return (
        lax.broadcasted_iota(jnp.int32, (H, H), 0),
        lax.broadcasted_iota(jnp.int32, (H, H), 1),
    )


def pack(out, a, p, b):
    r, c = grid_iota()
    out[0:N, :] = a
    out[N : N + H, 0:H] = p[H:, :H]
    out[N : N + H, H:] = jnp.where(r >= c, p[:H, :H], p[H:, H:])
    diag = jnp.sum(jnp.where(r == c, p[H:, H:], 0.0), axis=0, keepdims=True)
    row = lax.broadcasted_iota(jnp.int32, (8, N), 0)
    wide = jnp.concatenate([diag, diag], axis=1)
    out[N + H : N + H + 8, :] = jnp.where(row == 0, b, jnp.broadcast_to(wide, (8, N)))
    out[N + H + 8 :, :] = jnp.zeros((8, N), f32)


def unpack(ref):
    r, c = grid_iota()
    a = ref[0:N, :]
    x = ref[N : N + H, H:]
    tail = ref[N + H : N + H + 8, :]
    d2 = tail[1:2, :H]
    z11 = jnp.where(r > c, x, jnp.where(r == c, 0.5 * x, 0.0))
    z22 = jnp.where(r < c, x, jnp.where(r == c, 0.5 * jnp.broadcast_to(d2, (H, H)), 0.0))
    top = jnp.concatenate([z11, jnp.zeros((H, H), f32)], axis=1)
    low = jnp.concatenate([ref[N : N + H, :H], z22], axis=1)
    return a, jnp.concatenate([top, low], axis=0), jnp.broadcast_to(tail[0:1, :], (8, N))


def compose(later, earlier):
    a2 = split(later[0])
    a1, z1 = split(earlier[0]), split(earlier[1])
    a = mm3(a2, a1)
    z = mm3(split(mm3(a2, z1)), a2, 1, 1) + later[1]
    return a, z, row_times(earlier[2], a2) + later[2]


def apply_to(element, state):
    a = split(element[0])
    z = mm3(split(mm3(a, split(state[0]))), a, 1, 1) + element[1]
    return z, row_times(state[1], a) + element[2]


def local_kernel(t_ref, n_ref, f_ref, a_out, p_out, b_out, total):
    a = p = b = None
    for k in range(STEPS):
        noise = split(n_ref[k])
        q = mm3(noise, noise, 1, 1)
        push = jnp.broadcast_to(f_ref[k : k + 1, :], (8, N))
        if k == 0:
            a, p, b = t_ref[0], q, push
        else:
            t = split(t_ref[k])
            a = mm3(t, split(a))
            p = mm3(split(mm3(t, split(p))), t, 1, 1) + q
            b = row_times(b, t) + push
        a_out[k] = a
        p_out[k] = p
        b_out[k] = b
    pack(total, a, p, b)


def take_half(half, whole, c):
    half[...] = whole[pl.ds(pl.multiple_of(c * HALF, 8), HALF), :]


def core_kernel(place, own, other, half, total):
    c = place[3]

    def join(earlier, later):
        a, z, b = compose(unpack(later), unpack(earlier))
        pack(total, a, z + z.T, b)

    @pl.when(c == 0)
    def _():
        join(own, other)

    @pl.when(c == 1)
    def _():
        join(other, own)

    take_half(half, total, c)


def ring_kernel(which, place, own, r1, r2, r3, s1, s2, s3, half, total, ea, ez, eb, pieces):
    me, c = place[which], place[3]
    here = pl.multiple_of(c * HALF, 8)
    there = pl.multiple_of((1 - c) * HALF, 8)
    pieces[me] = own[...]
    for back, r, s in ((1, r1, s1), (2, r2, s2), (3, r3, s3)):
        spot = lax.rem(me + 4 - back, 4)
        pieces[spot, pl.ds(here, HALF), :] = r[...]
        pieces[spot, pl.ds(there, HALF), :] = s[...]
    state = unpack(pieces.at[0])
    eye = (
        lax.broadcasted_iota(jnp.int32, (N, N), 0) == lax.broadcasted_iota(jnp.int32, (N, N), 1)
    )
    ea[...] = jnp.where(eye, 1.0, 0.0)
    ez[...] = jnp.zeros((N, N), f32)
    eb[...] = jnp.zeros((8, N), f32)
    for p in range(1, 4):

        @pl.when(me == p)
        def _():
            ea[...] = state[0]
            ez[...] = state[1]
            eb[...] = state[2]

        state = compose(unpack(pieces.at[p]), state)
    a, z, b = state
    pack(total, a, z + z.T, b)
    take_half(half, total, c)


def lane(x, i):
    return jnp.take_along_axis(
        x, jnp.full(x.shape, i, jnp.int32), axis=1, mode="promise_in_bounds"
    )


def factor(rows, n):
    width = len(rows)

    def panel(q, _):
        j0 = q * PB
        held = [[ref[pl.ds((j0 + t) * 8, 8), :] for t in range(PB)] for ref in rows]
        for t in range(PB):
            inv = lax.rsqrt(lane(held[0][t], j0 + t))
            for w in range(width):
                held[w][t] = held[w][t] * inv
            for s in range(t + 1, PB):
                c = lane(held[0][t], j0 + s)
                for w in range(width):
                    held[w][s] = held[w][s] - c * held[w][t]
        for w in range(width):
            for t in range(PB):
                rows[w][pl.ds((j0 + t) * 8, 8), :] = held[w][t]

        def trail(p, _):
            i0 = p * PB
            for s in range(PB):
                acc = [rows[w][pl.ds((i0 + s) * 8, 8), :] for w in range(width)]
                for t in range(PB):
                    c = lane(held[0][t], i0 + s)
                    for w in range(width):
                        acc[w] = acc[w] - c * held[w][t]
                for w in range(width):
                    rows[w][pl.ds((i0 + s) * 8, 8), :] = acc[w]
            return 0

        lax.fori_loop(q + 1, n // PB, trail, 0)
        return 0

    lax.fori_loop(0, n // PB, panel, 0)


def strided(m):
    return pl.ds(m, H, stride=STEPS)


def cholesky(cov, l_ref, logs_ref, d1, b1, d2):
    for m in range(STEPS):
        d1[strided(m), :] = cov[m, 0:H, 0:H]
        b1[strided(m), :] = cov[m, 0:H, H:]
    factor([d1, b1], H)
    for m in range(STEPS):
        u = split(b1[strided(m), :])
        d2[strided(m), :] = cov[m, H:, H:] - mm3(u, u, 0, 0)
    factor([d2], H)
    r, c = grid_iota()
    total = jnp.zeros((1, H), f32)
    for m in range(STEPS):
        u1 = d1[strided(m), :]
        u2 = d2[strided(m), :]
        logs = jnp.log(jnp.where(r == c, u1, 1.0)) + jnp.log(jnp.where(r == c, u2, 1.0))
        total = total + jnp.sum(logs, axis=0, keepdims=True)
        l_ref[m, 0:H, 0:H] = jnp.where(r <= c, u1, 0.0).T
        l_ref[m, H:, 0:H] = b1[strided(m), :].T
        l_ref[m, H:, H:] = jnp.where(r <= c, u2, 0.0).T
        l_ref[m, 0:H, H:] = jnp.zeros((H, H), f32)
    logs_ref[...] = jnp.broadcast_to(total, (8, H))


def final_kernel(place, r1, r2, r3, s1, s2, s3, xa, xz, xb, ya, yz, yb, core, a_ref, p_ref, b_ref, m0_ref, l0_ref,
                 means, l_ref, logs, pieces, zs, ms, cov, d1, b1, d2):
    me, c = place[0], place[3]
    here = pl.multiple_of(c * HALF, 8)
    there = pl.multiple_of((1 - c) * HALF, 8)
    for back, r, s in ((1, r1, s1), (2, r2, s2), (3, r3, s3)):
        spot = lax.rem(me + 4 - back, 4)
        pieces[spot, pl.ds(here, HALF), :] = r[...]
        pieces[spot, pl.ds(there, HALF), :] = s[...]
    l0 = split(l0_ref[...])
    zs[...] = 0.5 * mm3(l0, l0, 1, 1)
    ms[...] = jnp.broadcast_to(m0_ref[...], (8, N))

    def slab(k, _):
        zs[...], ms[...] = apply_to(unpack(pieces.at[k]), (zs[...], ms[...]))
        return 0

    lax.fori_loop(0, me, slab, 0)
    for ea, ez, eb in ((xa, xz, xb), (ya, yz, yb)):
        zs[...], ms[...] = apply_to((ea[...], ez[...], eb[...]), (zs[...], ms[...]))

    @pl.when(c == 1)
    def _():
        zs[...], ms[...] = apply_to(unpack(core), (zs[...], ms[...]))

    z = zs[...]
    state = split(z + z.T)
    mean = ms[...]
    for k in range(STEPS):
        a = split(a_ref[k])
        cov[k] = mm3(split(mm3(a, state)), a, 1, 1) + p_ref[k]
        means[k : k + 1, :] = (row_times(mean, a) + b_ref[k])[0:1, :]
    cholesky(cov, l_ref, logs, d1, b1, d2)


VMEM = pl.BlockSpec(memory_space=pltpu.VMEM)
SMEM = pl.BlockSpec(memory_space=pltpu.SMEM)


def shape(*dims):
    return jax.ShapeDtypeStruct(dims, f32)


def call(kernel, outs, specs, scratch, name):
    return pl.pallas_call(
        kernel,
        out_shape=outs,
        in_specs=specs,
        out_specs=(VMEM,) * len(outs),
        scratch_shapes=scratch,
        compiler_params=pltpu.CompilerParams(vmem_limit_bytes=48 * 2**20),
        name=name,
    )


def ring(axis, back):
    stride, count = {"c": (1, 2), "y": (2, 4), "x": (8, 4), "z": (32, 4)}[axis]
    pairs = []
    for i in range(128):
        p = (i // stride) % count
        pairs.append((i, i + ((p + back) % count - p) * stride))
    return pairs


def send(x, axis, back):
    return lax.ppermute(x, AXES, ring(axis, back))


def gather_ring(half, axis):
    got = [send(half, axis, back) for back in (1, 2, 3)]
    return got + [send(g, "c", 1) for g in got]


def on_device(transitions, noise_factor, forcing, initial_mean, initial_factor):
    place = jnp.stack([lax.axis_index(axis) for axis in AXES]).astype(jnp.int32)
    stack = shape(STEPS, N, N)
    packed, half = shape(ROWS, N), shape(HALF, N)
    element = (shape(N, N), shape(N, N), shape(8, N))
    a, p, b, own = call(
        local_kernel, (stack, stack, shape(STEPS, 8, N), packed), [VMEM] * 3, [], "local"
    )(transitions, noise_factor, forcing)
    other = send(own, "c", 1)
    mine, total = call(core_kernel, (half, packed), [SMEM, VMEM, VMEM], [], "core")(place, own, other)
    before = []
    for axis, which in (("y", 2), ("x", 1)):
        mine, total, *earlier = call(
            lambda *refs, which=which: ring_kernel(which, *refs),
            (half, packed) + element,
            [SMEM] + [VMEM] * 7,
            [pltpu.VMEM((4, ROWS, N), f32)],
            "ring_" + axis,
        )(place, total, *gather_ring(mine, axis))
        before.append(earlier)
    by_y, by_x = before
    means, factors, logs = call(
        final_kernel,
        (shape(STEPS, N), stack, shape(8, H)),
        [SMEM] + [VMEM] * 18,
        [
            pltpu.VMEM((4, ROWS, N), f32),
            pltpu.VMEM((N, N), f32),
            pltpu.VMEM((8, N), f32),
            pltpu.VMEM((STEPS, N, N), f32),
            pltpu.VMEM((STEPS * H, H), f32),
            pltpu.VMEM((STEPS * H, H), f32),
            pltpu.VMEM((STEPS * H, H), f32),
        ],
        "final",
    )(place, *gather_ring(mine, "z"), *by_x, *by_y, other, a, p, b, initial_mean[None], initial_factor)
    logs = logs + send(logs, "c", 1)
    for axis in ("y", "x", "z"):
        one, two, three = [send(logs, axis, k) for k in (1, 2, 3)]
        logs = (logs + two) + (one + three)
    log_scale = jnp.sum(logs[0]) / (128 * STEPS * N)
    return means, factors, log_scale


def solution(mesh):
    cube = Mesh(mesh.devices.reshape(4, 4, 4, 2), AXES)
    return jax.shard_map(
        on_device,
        mesh=cube,
        in_specs=(P(AXES, None, None), P(AXES, None, None), P(AXES, None), P(), P()),
        out_specs=(P(AXES, None), P(AXES, None, None), P()),
        check_vma=False,
    )
```

```python
import jax
import jax.numpy as jnp
from jax import lax
from jax.experimental import pallas as pl
from jax.experimental.pallas import tpu as pltpu
from jax.sharding import Mesh, PartitionSpec as P

f32, bf16 = jnp.float32, jnp.bfloat16
AXES = ("z", "x", "y", "c")
N = 256
H = 128
STEPS = 8
ROWS = 400
HALF = ROWS // 2
PB = 8
NB = 32


def split(x):
    hi = x.astype(bf16)
    return hi, (x - hi.astype(f32)).astype(bf16)


def dg(a, b, ca, cb):
    return lax.dot_general(a, b, (((ca,), (cb,)), ((), ())), preferred_element_type=f32)


def mm3(a, b, ca=1, cb=0):
    return dg(a[0], b[0], ca, cb) + (dg(a[0], b[1], ca, cb) + dg(a[1], b[0], ca, cb))


def row_times(vec, a):
    v1 = vec.astype(bf16)
    rest = vec - v1.astype(f32)
    v2 = rest.astype(bf16)
    v3 = (rest - v2.astype(f32)).astype(bf16)
    out = dg(v3, a[0], 1, 1) + dg(v2, a[1], 1, 1)
    out = out + (dg(v2, a[0], 1, 1) + dg(v1, a[1], 1, 1))
    return out + dg(v1, a[0], 1, 1)


def grid_iota():
    return (
        lax.broadcasted_iota(jnp.int32, (H, H), 0),
        lax.broadcasted_iota(jnp.int32, (H, H), 1),
    )


def pack(out, a, p, b):
    r, c = grid_iota()
    out[0:N, :] = a
    out[N : N + H, 0:H] = p[H:, :H]
    out[N : N + H, H:] = jnp.where(r >= c, p[:H, :H], p[H:, H:])
    diag = jnp.sum(jnp.where(r == c, p[H:, H:], 0.0), axis=0, keepdims=True)
    row = lax.broadcasted_iota(jnp.int32, (8, N), 0)
    wide = jnp.concatenate([diag, diag], axis=1)
    out[N + H : N + H + 8, :] = jnp.where(row == 0, b, jnp.broadcast_to(wide, (8, N)))
    out[N + H + 8 :, :] = jnp.zeros((8, N), f32)


def unpack(ref):
    r, c = grid_iota()
    a = ref[0:N, :]
    x = ref[N : N + H, H:]
    tail = ref[N + H : N + H + 8, :]
    d2 = tail[1:2, :H]
    z11 = jnp.where(r > c, x, jnp.where(r == c, 0.5 * x, 0.0))
    z22 = jnp.where(r < c, x, jnp.where(r == c, 0.5 * jnp.broadcast_to(d2, (H, H)), 0.0))
    top = jnp.concatenate([z11, jnp.zeros((H, H), f32)], axis=1)
    low = jnp.concatenate([ref[N : N + H, :H], z22], axis=1)
    return a, jnp.concatenate([top, low], axis=0), jnp.broadcast_to(tail[0:1, :], (8, N))


def compose(later, earlier):
    a2 = split(later[0])
    a1, z1 = split(earlier[0]), split(earlier[1])
    a = mm3(a2, a1)
    z = mm3(split(mm3(a2, z1)), a2, 1, 1) + later[1]
    return a, z, row_times(earlier[2], a2) + later[2]


def apply_to(element, state):
    a = split(element[0])
    z = mm3(split(mm3(a, split(state[0]))), a, 1, 1) + element[1]
    return z, row_times(state[1], a) + element[2]


def local_kernel(t_ref, n_ref, f_ref, a_out, p_out, b_out, total):
    a = p = b = None
    for k in range(STEPS):
        noise = split(n_ref[k])
        q = mm3(noise, noise, 1, 1)
        push = jnp.broadcast_to(f_ref[k : k + 1, :], (8, N))
        if k == 0:
            a, p, b = t_ref[0], q, push
        else:
            t = split(t_ref[k])
            a = mm3(t, split(a))
            p = mm3(split(mm3(t, split(p))), t, 1, 1) + q
            b = row_times(b, t) + push
        a_out[k] = a
        p_out[k] = p
        b_out[k] = b
    pack(total, a, p, b)


def take_half(half, whole, c):
    half[...] = whole[pl.ds(pl.multiple_of(c * HALF, 8), HALF), :]


def core_kernel(place, own, other, half, total):
    c = place[3]

    def join(earlier, later):
        a, z, b = compose(unpack(later), unpack(earlier))
        pack(total, a, z + z.T, b)

    @pl.when(c == 0)
    def _():
        join(own, other)

    @pl.when(c == 1)
    def _():
        join(other, own)

    take_half(half, total, c)


def ring_kernel(which, place, own, r1, r2, r3, s1, s2, s3, half, total, ea, ez, eb, pieces):
    me, c = place[which], place[3]
    here = pl.multiple_of(c * HALF, 8)
    there = pl.multiple_of((1 - c) * HALF, 8)
    pieces[me] = own[...]
    for back, r, s in ((1, r1, s1), (2, r2, s2), (3, r3, s3)):
        spot = lax.rem(me + 4 - back, 4)
        pieces[spot, pl.ds(here, HALF), :] = r[...]
        pieces[spot, pl.ds(there, HALF), :] = s[...]
    state = unpack(pieces.at[0])
    eye = (
        lax.broadcasted_iota(jnp.int32, (N, N), 0) == lax.broadcasted_iota(jnp.int32, (N, N), 1)
    )
    ea[...] = jnp.where(eye, 1.0, 0.0)
    ez[...] = jnp.zeros((N, N), f32)
    eb[...] = jnp.zeros((8, N), f32)
    for p in range(1, 4):

        @pl.when(me == p)
        def _():
            ea[...] = state[0]
            ez[...] = state[1]
            eb[...] = state[2]

        state = compose(unpack(pieces.at[p]), state)
    a, z, b = state
    pack(total, a, z + z.T, b)
    take_half(half, total, c)


def lane(x, i):
    return jnp.broadcast_to(x[:, i : i + 1], x.shape)


def factor_block(rows, o):
    tiles, count = len(rows), len(rows[0])
    for q in range(0, count, PB):
        a = {(t, s): lane(rows[0][q + t], o + q + s) for t in range(PB) for s in range(t, PB)}
        for t in range(PB):
            inv = lax.rsqrt(a[t, t])
            u = {s: a[t, s] * inv for s in range(t + 1, PB)}
            for s in range(t + 1, PB):
                for r in range(s, PB):
                    a[s, r] = a[s, r] - u[s] * u[r]
            for w in range(tiles):
                rows[w][q + t] = rows[w][q + t] * inv
                for s in range(t + 1, PB):
                    rows[w][q + s] = rows[w][q + s] - u[s] * rows[w][q + t]
        for i in range(q + PB, count):
            for t in range(PB):
                c = lane(rows[0][q + t], o + i)
                for w in range(tiles):
                    rows[w][i] = rows[w][i] - c * rows[w][q + t]


def strided(j, count, m):
    return pl.ds(STEPS * j + m, count, stride=STEPS)


def cholesky(cov, l_ref, logs_ref, u0, u1):
    us = (u0, u1)
    for j0 in range(0, N, NB):
        first, r0 = j0 // H, j0 + NB
        tiles = range(first, 2)
        for m in range(STEPS):
            for w in tiles:
                us[w][strided(j0, NB, m), :] = cov[m, j0:r0, H * w : H * w + H]
        rows = [[us[w][pl.ds(8 * (j0 + i), 8), :] for i in range(NB)] for w in tiles]
        factor_block(rows, j0 % H)
        for w in tiles:
            for i in range(NB):
                us[w][pl.ds(8 * (j0 + i), 8), :] = rows[w - first][i]
        if r0 == N:
            break
        for m in range(STEPS):
            u = jnp.concatenate([us[w][strided(j0, NB, m), :] for w in tiles], axis=1)
            left, right = split(u.T[r0 - H * first :, :]), split(u)
            cov[m, r0:, H * first :] = cov[m, r0:, H * first :] - mm3(left, right)
    r, c = grid_iota()
    total = jnp.zeros((1, H), f32)
    for m in range(STEPS):
        a1 = u0[strided(0, H, m), :]
        a2 = u1[strided(H, H, m), :]
        logs = jnp.log(jnp.where(r == c, a1, 1.0)) + jnp.log(jnp.where(r == c, a2, 1.0))
        total = total + jnp.sum(logs, axis=0, keepdims=True)
        l_ref[m, 0:H, 0:H] = jnp.where(r <= c, a1, 0.0).T
        l_ref[m, H:, 0:H] = u1[strided(0, H, m), :].T
        l_ref[m, H:, H:] = jnp.where(r <= c, a2, 0.0).T
        l_ref[m, 0:H, H:] = jnp.zeros((H, H), f32)
    logs_ref[...] = jnp.broadcast_to(total, (8, H))


def final_kernel(place, r1, r2, r3, s1, s2, s3, xa, xz, xb, ya, yz, yb, core, a_ref, p_ref, b_ref, m0_ref, l0_ref,
                 means, l_ref, logs, pieces, zs, ms, cov, u0, u1):
    me, c = place[0], place[3]
    here = pl.multiple_of(c * HALF, 8)
    there = pl.multiple_of((1 - c) * HALF, 8)
    for back, r, s in ((1, r1, s1), (2, r2, s2), (3, r3, s3)):
        spot = lax.rem(me + 4 - back, 4)
        pieces[spot, pl.ds(here, HALF), :] = r[...]
        pieces[spot, pl.ds(there, HALF), :] = s[...]
    l0 = split(l0_ref[...])
    zs[...] = 0.5 * mm3(l0, l0, 1, 1)
    ms[...] = jnp.broadcast_to(m0_ref[...], (8, N))

    def slab(k, _):
        zs[...], ms[...] = apply_to(unpack(pieces.at[k]), (zs[...], ms[...]))
        return 0

    lax.fori_loop(0, me, slab, 0)
    for ea, ez, eb in ((xa, xz, xb), (ya, yz, yb)):
        zs[...], ms[...] = apply_to((ea[...], ez[...], eb[...]), (zs[...], ms[...]))

    @pl.when(c == 1)
    def _():
        zs[...], ms[...] = apply_to(unpack(core), (zs[...], ms[...]))

    z = zs[...]
    state = split(z + z.T)
    mean = ms[...]
    for k in range(STEPS):
        a = split(a_ref[k])
        cov[k] = mm3(split(mm3(a, state)), a, 1, 1) + p_ref[k]
        means[k : k + 1, :] = (row_times(mean, a) + b_ref[k])[0:1, :]
    cholesky(cov, l_ref, logs, u0, u1)


VMEM = pl.BlockSpec(memory_space=pltpu.VMEM)
SMEM = pl.BlockSpec(memory_space=pltpu.SMEM)


def shape(*dims):
    return jax.ShapeDtypeStruct(dims, f32)


def call(kernel, outs, specs, scratch, name):
    return pl.pallas_call(
        kernel,
        out_shape=outs,
        in_specs=specs,
        out_specs=(VMEM,) * len(outs),
        scratch_shapes=scratch,
        compiler_params=pltpu.CompilerParams(vmem_limit_bytes=48 * 2**20),
        name=name,
    )


def ring(axis, back):
    stride, count = {"c": (1, 2), "y": (2, 4), "x": (8, 4), "z": (32, 4)}[axis]
    pairs = []
    for i in range(128):
        p = (i // stride) % count
        pairs.append((i, i + ((p + back) % count - p) * stride))
    return pairs


def send(x, axis, back):
    return lax.ppermute(x, AXES, ring(axis, back))


def gather_ring(half, axis):
    got = [send(half, axis, back) for back in (1, 2, 3)]
    return got + [send(g, "c", 1) for g in got]


def on_device(transitions, noise_factor, forcing, initial_mean, initial_factor):
    place = jnp.stack([lax.axis_index(axis) for axis in AXES]).astype(jnp.int32)
    stack = shape(STEPS, N, N)
    packed, half = shape(ROWS, N), shape(HALF, N)
    element = (shape(N, N), shape(N, N), shape(8, N))
    a, p, b, own = call(
        local_kernel, (stack, stack, shape(STEPS, 8, N), packed), [VMEM] * 3, [], "local"
    )(transitions, noise_factor, forcing)
    other = send(own, "c", 1)
    mine, total = call(core_kernel, (half, packed), [SMEM, VMEM, VMEM], [], "core")(place, own, other)
    before = []
    for axis, which in (("y", 2), ("x", 1)):
        mine, total, *earlier = call(
            lambda *refs, which=which: ring_kernel(which, *refs),
            (half, packed) + element,
            [SMEM] + [VMEM] * 7,
            [pltpu.VMEM((4, ROWS, N), f32)],
            "ring_" + axis,
        )(place, total, *gather_ring(mine, axis))
        before.append(earlier)
    by_y, by_x = before
    means, factors, logs = call(
        final_kernel,
        (shape(STEPS, N), stack, shape(8, H)),
        [SMEM] + [VMEM] * 18,
        [
            pltpu.VMEM((4, ROWS, N), f32),
            pltpu.VMEM((N, N), f32),
            pltpu.VMEM((8, N), f32),
            pltpu.VMEM((STEPS, N, N), f32),
            pltpu.VMEM((STEPS * N, H), f32),
            pltpu.VMEM((STEPS * N, H), f32),
        ],
        "final",
    )(place, *gather_ring(mine, "z"), *by_x, *by_y, other, a, p, b, initial_mean[None], initial_factor)
    logs = logs + send(logs, "c", 1)
    for axis in ("y", "x", "z"):
        one, two, three = [send(logs, axis, k) for k in (1, 2, 3)]
        logs = (logs + two) + (one + three)
    log_scale = jnp.sum(logs[0]) / (128 * STEPS * N)
    return means, factors, log_scale


def solution(mesh):
    cube = Mesh(mesh.devices.reshape(4, 4, 4, 2), AXES)
    return jax.shard_map(
        on_device,
        mesh=cube,
        in_specs=(P(AXES, None, None), P(AXES, None, None), P(AXES, None), P(), P()),
        out_specs=(P(AXES, None), P(AXES, None, None), P()),
        check_vma=False,
    )
```

```python
import jax
import jax.numpy as jnp
from jax import lax
from jax.experimental import pallas as pl
from jax.experimental.pallas import tpu as pltpu
from jax.sharding import Mesh, PartitionSpec as P

f32, bf16 = jnp.float32, jnp.bfloat16
AXES = ("z", "x", "y", "c")
N = 256
H = 128
STEPS = 8
ROWS = 400
HALF = ROWS // 2
PB = 8
NB = 32


def split(x):
    hi = x.astype(bf16)
    return hi, (x - hi.astype(f32)).astype(bf16)


def dg(a, b, ca, cb):
    return lax.dot_general(a, b, (((ca,), (cb,)), ((), ())), preferred_element_type=f32)


def mm3(a, b, ca=1, cb=0):
    small = dg(a[0], b[1], ca, cb) + dg(a[1], b[0], ca, cb)
    return dg(a[0], b[0], ca, cb) + (small + dg(a[1], b[1], ca, cb))


def row_times(vec, a):
    v1 = vec.astype(bf16)
    rest = vec - v1.astype(f32)
    v2 = rest.astype(bf16)
    v3 = (rest - v2.astype(f32)).astype(bf16)
    out = dg(v3, a[0], 1, 1) + dg(v2, a[1], 1, 1)
    out = out + (dg(v2, a[0], 1, 1) + dg(v1, a[1], 1, 1))
    return out + dg(v1, a[0], 1, 1)


def grid_iota():
    return (
        lax.broadcasted_iota(jnp.int32, (H, H), 0),
        lax.broadcasted_iota(jnp.int32, (H, H), 1),
    )


def pack(out, a, p, b):
    r, c = grid_iota()
    out[0:N, :] = a
    out[N : N + H, 0:H] = p[H:, :H]
    out[N : N + H, H:] = jnp.where(r >= c, p[:H, :H], p[H:, H:])
    diag = jnp.sum(jnp.where(r == c, p[H:, H:], 0.0), axis=0, keepdims=True)
    row = lax.broadcasted_iota(jnp.int32, (8, N), 0)
    wide = jnp.concatenate([diag, diag], axis=1)
    out[N + H : N + H + 8, :] = jnp.where(row == 0, b, jnp.broadcast_to(wide, (8, N)))
    out[N + H + 8 :, :] = jnp.zeros((8, N), f32)


def unpack(ref):
    r, c = grid_iota()
    a = ref[0:N, :]
    x = ref[N : N + H, H:]
    tail = ref[N + H : N + H + 8, :]
    d2 = tail[1:2, :H]
    z11 = jnp.where(r > c, x, jnp.where(r == c, 0.5 * x, 0.0))
    z22 = jnp.where(r < c, x, jnp.where(r == c, 0.5 * jnp.broadcast_to(d2, (H, H)), 0.0))
    top = jnp.concatenate([z11, jnp.zeros((H, H), f32)], axis=1)
    low = jnp.concatenate([ref[N : N + H, :H], z22], axis=1)
    return a, jnp.concatenate([top, low], axis=0), jnp.broadcast_to(tail[0:1, :], (8, N))


class Step:
    def __init__(self, a, cov, b):
        self.a, self.cov, self.b = a, cov, b
        self.a2, self.cov2 = split(a), split(cov)

    def after(self, earlier):
        a = mm3(self.a2, earlier.a2)
        cov = mm3(split(mm3(self.a2, earlier.cov2)), self.a2, 1, 1) + self.cov
        return Step(a, cov, row_times(earlier.b, self.a2) + self.b)


def apply_to(step, state):
    z = mm3(split(mm3(step.a2, split(state[0]))), step.a2, 1, 1) + step.cov
    return z, row_times(state[1], step.a2) + step.b


def one_step(t_ref, n_ref, f_ref, k):
    noise = split(n_ref[k])
    push = jnp.broadcast_to(f_ref[k : k + 1, :], (8, N))
    return Step(t_ref[k], mm3(noise, noise, 1, 1), push)


def local_kernel(t_ref, n_ref, f_ref, total):
    level = [one_step(t_ref, n_ref, f_ref, k) for k in range(STEPS)]
    while len(level) > 1:
        level = [level[k + 1].after(level[k]) for k in range(0, len(level), 2)]
    pack(total, level[0].a, level[0].cov, level[0].b)


def prefix_kernel(t_ref, n_ref, f_ref, later, a_out, p_out, b_out):
    def put(k, step):
        a_out[k], p_out[k], b_out[k] = step.a, step.cov, step.b

    g = [one_step(t_ref, n_ref, f_ref, k) for k in range(STEPS)]
    pairs = [g[k + 1].after(g[k]) for k in range(0, STEPS, 2)]
    front, back = pairs[1].after(pairs[0]), pairs[3].after(pairs[2])
    put(0, g[0])
    put(1, pairs[0])
    put(2, g[2].after(pairs[0]))
    put(3, front)
    put(4, g[4].after(front))
    six = pairs[2].after(front)
    put(5, six)
    put(6, g[6].after(six))
    put(7, back.after(front))


def take_half(half, whole, c):
    half[...] = whole[pl.ds(pl.multiple_of(c * HALF, 8), HALF), :]


def core_kernel(place, own, other, half, total):
    c = place[3]
    mine, theirs = unpack(own), unpack(other)
    earlier = Step(*[jnp.where(c == 0, u, v) for u, v in zip(mine, theirs)])
    later = Step(*[jnp.where(c == 0, v, u) for u, v in zip(mine, theirs)])
    both = later.after(earlier)
    pack(total, both.a, both.cov + both.cov.T, both.b)
    take_half(half, total, c)


def stack_kernel(r1, r2, r3, beside, out):
    for k, r in enumerate((r1, r2, r3)):
        out[k] = r[...]


def lay_out(pieces, place, which, direct, passed):
    me, c = place[which], place[3]
    here = pl.multiple_of(c * HALF, 8)
    there = pl.multiple_of((1 - c) * HALF, 8)
    for back in (1, 2, 3):
        spot = lax.rem(me + 4 - back, 4)
        pieces[spot, pl.ds(here, HALF), :] = direct[back - 1]
        pieces[spot, pl.ds(there, HALF), :] = passed[back - 1]


def neutral():
    rows = lax.broadcasted_iota(jnp.int32, (N, N), 0)
    columns = lax.broadcasted_iota(jnp.int32, (N, N), 1)
    eye = jnp.where(rows == columns, 1.0, 0.0)
    return eye, jnp.zeros((N, N), f32), jnp.zeros((8, N), f32)


def ring_kernel(which, place, own, direct, passed, half, total, ea, ez, eb, pieces):
    me, c = place[which], place[3]
    pieces[me] = own[...]
    lay_out(pieces, place, which, direct, passed)
    g = [Step(*unpack(pieces.at[k])) for k in range(4)]
    front, back = g[1].after(g[0]), g[3].after(g[2])
    whole = back.after(front)
    pack(total, whole.a, whole.cov + whole.cov.T, whole.b)
    take_half(half, total, c)
    three = g[2].after(front)
    before = (neutral(),) + tuple((e.a, e.cov, e.b) for e in (g[0], front, three))
    for k in range(4):

        @pl.when(me == k)
        def _():
            ea[...], ez[...], eb[...] = before[k]


def join_kernel(place, xa, xz, xb, ya, yz, yb, core, ea, ez, eb):
    c = place[3]
    last = Step(*[jnp.where(c == 1, u, v) for u, v in zip(unpack(core), neutral())])
    by_x, by_y = Step(xa[...], xz[...], xb[...]), Step(ya[...], yz[...], yb[...])
    both = last.after(by_y).after(by_x)
    ea[...], ez[...], eb[...] = both.a, both.cov, both.b


def lane(x, i):
    return jnp.broadcast_to(x[:, i : i + 1], x.shape)


def factor_block(rows, o):
    tiles, count = len(rows), len(rows[0])
    for q in range(0, count, PB):
        a = {(t, s): lane(rows[0][q + t], o + q + s) for t in range(PB) for s in range(t, PB)}
        for t in range(PB):
            inv = lax.rsqrt(a[t, t])
            u = {s: a[t, s] * inv for s in range(t + 1, PB)}
            for s in range(t + 1, PB):
                for r in range(s, PB):
                    a[s, r] = a[s, r] - u[s] * u[r]
            for w in range(tiles):
                rows[w][q + t] = rows[w][q + t] * inv
                for s in range(t + 1, PB):
                    rows[w][q + s] = rows[w][q + s] - u[s] * rows[w][q + t]
        for i in range(q + PB, count):
            for t in range(PB):
                c = lane(rows[0][q + t], o + i)
                for w in range(tiles):
                    rows[w][i] = rows[w][i] - c * rows[w][q + t]


def strided(j, count, m):
    return pl.ds(STEPS * j + m, count, stride=STEPS)


def cholesky(cov, l_ref, logs_ref, u0, u1):
    us = (u0, u1)
    for j0 in range(0, N, NB):
        first, r0 = j0 // H, j0 + NB
        tiles = range(first, 2)
        for m in range(STEPS):
            for w in tiles:
                us[w][strided(j0, NB, m), :] = cov[m, j0:r0, H * w : H * w + H]
        rows = [[us[w][pl.ds(8 * (j0 + i), 8), :] for i in range(NB)] for w in tiles]
        factor_block(rows, j0 % H)
        for w in tiles:
            for i in range(NB):
                us[w][pl.ds(8 * (j0 + i), 8), :] = rows[w - first][i]
        if r0 == N:
            break
        for m in range(STEPS):
            u = jnp.concatenate([us[w][strided(j0, NB, m), :] for w in tiles], axis=1)
            left, right = split(u.T[r0 - H * first :, :]), split(u)
            cov[m, r0:, H * first :] = cov[m, r0:, H * first :] - mm3(left, right)
    r, c = grid_iota()
    diagonals = []
    for m in range(STEPS):
        a1 = u0[strided(0, H, m), :]
        a2 = u1[strided(H, H, m), :]
        diagonals += [jnp.sum(jnp.where(r == c, u, 0.0), axis=0, keepdims=True) for u in (a1, a2)]
        l_ref[m, 0:H, 0:H] = jnp.where(r <= c, a1, 0.0).T
        l_ref[m, H:, 0:H] = u1[strided(0, H, m), :].T
        l_ref[m, H:, H:] = jnp.where(r <= c, a2, 0.0).T
        l_ref[m, 0:H, H:] = jnp.zeros((H, H), f32)
    logs = jnp.sum(jnp.log(jnp.concatenate(diagonals, axis=0)), axis=0, keepdims=True)
    logs_ref[...] = jnp.broadcast_to(jnp.sum(logs, axis=1, keepdims=True), (1, H))


def final_kernel(place, direct, passed, ea, ez, eb, a_ref, p_ref, b_ref, m0_ref, l0_ref,
                 means, l_ref, logs, pieces, zs, ms, cov, u0, u1):
    lay_out(pieces, place, 0, direct, passed)
    l0 = split(l0_ref[...])
    zs[...] = 0.5 * mm3(l0, l0, 1, 1)
    ms[...] = jnp.broadcast_to(m0_ref[...], (8, N))

    def slab(k, _):
        zs[...], ms[...] = apply_to(Step(*unpack(pieces.at[k])), (zs[...], ms[...]))
        return 0

    lax.fori_loop(0, place[0], slab, 0)
    z, mean = apply_to(Step(ea[...], ez[...], eb[...]), (zs[...], ms[...]))
    state = split(z + z.T)
    for k in range(STEPS):
        a = split(a_ref[k])
        cov[k] = mm3(split(mm3(a, state)), a, 1, 1) + p_ref[k]
        means[k : k + 1, :] = (row_times(mean, a) + b_ref[k])[0:1, :]
    cholesky(cov, l_ref, logs, u0, u1)


VMEM = pl.BlockSpec(memory_space=pltpu.VMEM)
ANY = pl.BlockSpec(memory_space=pl.ANY)
SMEM = pl.BlockSpec(memory_space=pltpu.SMEM)


def shape(*dims):
    return jax.ShapeDtypeStruct(dims, f32)


def call(kernel, outs, specs, scratch, name, mib, products):
    return pl.pallas_call(
        kernel,
        out_shape=outs,
        in_specs=specs,
        out_specs=(VMEM,) * len(outs),
        scratch_shapes=scratch,
        compiler_params=pltpu.CompilerParams(vmem_limit_bytes=mib * 2**20),
        cost_estimate=pl.CostEstimate(
            flops=products * 6 * N**3, bytes_accessed=8 * N * N * products, transcendentals=0
        ),
        name=name,
    )


def ring(axis, back):
    stride, count = {"c": (1, 2), "y": (2, 4), "x": (8, 4), "z": (32, 4)}[axis]
    pairs = []
    for i in range(128):
        p = (i // stride) % count
        pairs.append((i, i + ((p + back) % count - p) * stride))
    return pairs


def send(x, axis, back):
    return lax.ppermute(x, AXES, ring(axis, back))


def gather_ring(half, axis, beside):
    got = [send(half, axis, back) for back in (1, 2, 3)]
    direct = call(stack_kernel, (shape(3, HALF, N),), [VMEM] * 3 + [ANY], [], "stack_" + axis, 8, 1)(
        *got, beside
    )[0]
    return direct, send(direct, "c", 1)


def on_device(transitions, noise_factor, forcing, initial_mean, initial_factor):
    place = jnp.stack([lax.axis_index(axis) for axis in AXES]).astype(jnp.int32)
    stack = shape(STEPS, N, N)
    packed, half = shape(ROWS, N), shape(HALF, N)
    element = (shape(N, N), shape(N, N), shape(8, N))
    own = call(local_kernel, (packed,), [VMEM] * 3, [], "local", 24, 29)(
        transitions, noise_factor, forcing
    )[0]
    other = send(own, "c", 1)
    mine, total = call(core_kernel, (half, packed), [SMEM, VMEM, VMEM], [], "core", 12, 3)(
        place, own, other
    )
    a, p, b = call(
        prefix_kernel, (stack, stack, shape(STEPS, 8, N)), [VMEM] * 3 + [ANY], [], "prefix", 24, 47
    )(transitions, noise_factor, forcing, total)
    before = []
    for axis, which, beside in (("y", 2, b), ("x", 1, place)):
        mine, total, *earlier = call(
            lambda *refs, which=which: ring_kernel(which, *refs),
            (half, packed) + element,
            [SMEM] + [VMEM] * 3,
            [pltpu.VMEM((4, ROWS, N), f32)],
            "ring_" + axis,
            16,
            12,
        )(place, total, *gather_ring(mine, axis, beside))
        before.append(earlier)
    by_y, by_x = before
    entry = call(join_kernel, element, [SMEM] + [VMEM] * 7, [], "join", 12, 6)(
        place, *by_x, *by_y, other
    )
    means, factors, logs = call(
        final_kernel,
        (shape(STEPS, N), stack, shape(1, H)),
        [SMEM] + [VMEM] * 10,
        [
            pltpu.VMEM((4, ROWS, N), f32),
            pltpu.VMEM((N, N), f32),
            pltpu.VMEM((8, N), f32),
            pltpu.VMEM((STEPS, N, N), f32),
            pltpu.VMEM((STEPS * N, H), f32),
            pltpu.VMEM((STEPS * N, H), f32),
        ],
        "final",
        24,
        32,
    )(place, *gather_ring(mine, "z", entry[2]), *entry, a, p, b, initial_mean[None], initial_factor)
    logs = lax.all_to_all(logs.reshape(H), AXES, 0, 0, tiled=True)
    log_scale = jnp.sum(logs) / (128 * STEPS * N)
    return means, factors, log_scale


def solution(mesh):
    cube = Mesh(mesh.devices.reshape(4, 4, 4, 2), AXES)
    return jax.shard_map(
        on_device,
        mesh=cube,
        in_specs=(P(AXES, None, None), P(AXES, None, None), P(AXES, None), P(), P()),
        out_specs=(P(AXES, None), P(AXES, None, None), P()),
        check_vma=False,
    )
```

```python
import jax
import jax.numpy as jnp
from jax import lax
from jax.experimental import pallas as pl
from jax.experimental.pallas import tpu as pltpu
from jax.sharding import Mesh, PartitionSpec as P

f32, bf16 = jnp.float32, jnp.bfloat16
AXES = ("z", "x", "y", "c")
N = 256
H = 128
STEPS = 8
ROWS = 400
HALF = ROWS // 2
PB = 8
NB = 32


def split(x):
    hi = x.astype(bf16)
    return hi, (x - hi.astype(f32)).astype(bf16)


def dg(a, b, ca, cb):
    return lax.dot_general(a, b, (((ca,), (cb,)), ((), ())), preferred_element_type=f32)


def mm3(a, b, ca=1, cb=0):
    return dg(a[0], b[0], ca, cb) + (dg(a[0], b[1], ca, cb) + dg(a[1], b[0], ca, cb))


def mm4(a, b):
    return dg(a[0], b[0], 1, 0) + ((dg(a[0], b[1], 1, 0) + dg(a[1], b[0], 1, 0)) + dg(a[1], b[1], 1, 0))


def through(a, cov, b):
    high, low = split(mm3(a, cov))
    wide = jnp.concatenate([b, b], axis=0)
    v1 = wide.astype(bf16)
    rest = wide - v1.astype(f32)
    v2 = rest.astype(bf16)
    v3 = (rest - v2.astype(f32)).astype(bf16)
    by_high = dg(jnp.concatenate([high, low, v1, v2, v3], axis=0), a[0], 1, 1)
    by_low = dg(jnp.concatenate([high, v1, v2], axis=0), a[1], 1, 1)
    out = by_high[:N] + (by_high[N : 2 * N] + by_low[:N])
    vec = by_high[2 * N + 32 : 2 * N + 40] + by_low[N + 16 : N + 24]
    vec = vec + (by_high[2 * N + 16 : 2 * N + 24] + by_low[N : N + 8])
    return out, by_high[2 * N : 2 * N + 8] + vec


def grid_iota():
    return (
        lax.broadcasted_iota(jnp.int32, (H, H), 0),
        lax.broadcasted_iota(jnp.int32, (H, H), 1),
    )


def pack(out, a, p, b):
    r, c = grid_iota()
    out[0:N, :] = a
    out[N : N + H, 0:H] = p[H:, :H]
    out[N : N + H, H:] = jnp.where(r >= c, p[:H, :H], p[H:, H:])
    diag = jnp.sum(jnp.where(r == c, p[H:, H:], 0.0), axis=0, keepdims=True)
    row = lax.broadcasted_iota(jnp.int32, (8, N), 0)
    wide = jnp.concatenate([diag, diag], axis=1)
    out[N + H : N + H + 8, :] = jnp.where(row == 0, b, jnp.broadcast_to(wide, (8, N)))
    out[N + H + 8 :, :] = jnp.zeros((8, N), f32)


def unpack(ref):
    r, c = grid_iota()
    a = ref[0:N, :]
    x = ref[N : N + H, H:]
    tail = ref[N + H : N + H + 8, :]
    d2 = tail[1:2, :H]
    z11 = jnp.where(r > c, x, jnp.where(r == c, 0.5 * x, 0.0))
    z22 = jnp.where(r < c, x, jnp.where(r == c, 0.5 * jnp.broadcast_to(d2, (H, H)), 0.0))
    top = jnp.concatenate([z11, jnp.zeros((H, H), f32)], axis=1)
    low = jnp.concatenate([ref[N : N + H, :H], z22], axis=1)
    return a, jnp.concatenate([top, low], axis=0), jnp.broadcast_to(tail[0:1, :], (8, N))


class Step:
    def __init__(self, a, cov, b):
        self.a, self.cov, self.b = a, cov, b
        self.a2, self.cov2 = split(a), split(cov)

    def after(self, earlier):
        cov, b = through(self.a2, earlier.cov2, earlier.b)
        return Step(mm4(self.a2, earlier.a2), cov + self.cov, b + self.b)


def apply_to(step, state):
    z, m = through(step.a2, split(state[0]), state[1])
    return z + step.cov, m + step.b


def fetch(t_hbm, n_hbm, f_hbm, t_buf, n_buf, f_buf, sems, f_sem):
    copies = []
    pushes = pltpu.make_async_copy(f_hbm, f_buf, f_sem)
    pushes.start()
    for k in range(STEPS):
        pair = [
            pltpu.make_async_copy(n_hbm.at[k], n_buf.at[k], sems.at[k, 0]),
            pltpu.make_async_copy(t_hbm.at[k], t_buf.at[k], sems.at[k, 1]),
        ]
        for copy in pair:
            copy.start()
        copies.append(pair)

    pushes.wait()

    def one(k):
        for copy in copies[k]:
            copy.wait()
        noise = split(n_buf[k])
        push = jnp.broadcast_to(f_buf[k : k + 1, :], (8, N))
        return Step(t_buf[k], mm3(noise, noise, 1, 1), push)

    return one


def local_kernel(t_hbm, n_hbm, f_hbm, total, *buffers):
    one = fetch(t_hbm, n_hbm, f_hbm, *buffers)
    pairs = []
    for k in range(0, STEPS, 2):
        earlier, later = one(k), one(k + 1)
        pairs.append(later.after(earlier))
    whole = pairs[3].after(pairs[2]).after(pairs[1].after(pairs[0]))
    pack(total, whole.a, whole.cov, whole.b)


def prefix_kernel(t_hbm, n_hbm, f_hbm, later, a_out, p_out, b_out, *buffers):
    one = fetch(t_hbm, n_hbm, f_hbm, *buffers)

    def put(k, step):
        a_out[k], p_out[k], b_out[k] = step.a, step.cov, step.b

    g, pairs = [], []
    for k in range(0, STEPS, 2):
        g += [one(k), one(k + 1)]
        pairs.append(g[k + 1].after(g[k]))
    put(0, g[0])
    put(1, pairs[0])
    put(2, g[2].after(pairs[0]))
    front = pairs[1].after(pairs[0])
    put(3, front)
    put(4, g[4].after(front))
    six = pairs[2].after(front)
    put(5, six)
    put(6, g[6].after(six))
    put(7, pairs[3].after(six))


def take_half(half, whole, c):
    half[...] = whole[pl.ds(pl.multiple_of(c * HALF, 8), HALF), :]


def core_kernel(place, own, other, half, total):
    c = place[3]
    mine, theirs = unpack(own), unpack(other)
    earlier = Step(*[jnp.where(c == 0, u, v) for u, v in zip(mine, theirs)])
    later = Step(*[jnp.where(c == 0, v, u) for u, v in zip(mine, theirs)])
    both = later.after(earlier)
    pack(total, both.a, both.cov + both.cov.T, both.b)
    take_half(half, total, c)


def stack_kernel(r1, r2, r3, beside, out):
    for k, r in enumerate((r1, r2, r3)):
        out[k] = r[...]


def lay_out(pieces, place, which, direct, passed):
    me, c = place[which], place[3]
    here = pl.multiple_of(c * HALF, 8)
    there = pl.multiple_of((1 - c) * HALF, 8)
    for back in (1, 2, 3):
        spot = lax.rem(me + 4 - back, 4)
        pieces[spot, pl.ds(here, HALF), :] = direct[back - 1]
        pieces[spot, pl.ds(there, HALF), :] = passed[back - 1]


def neutral():
    rows = lax.broadcasted_iota(jnp.int32, (N, N), 0)
    columns = lax.broadcasted_iota(jnp.int32, (N, N), 1)
    eye = jnp.where(rows == columns, 1.0, 0.0)
    return eye, jnp.zeros((N, N), f32), jnp.zeros((8, N), f32)


def ring_kernel(which, place, own, direct, passed, half, total, pieces):
    pieces[place[which]] = own[...]
    lay_out(pieces, place, which, direct, passed)
    g = [Step(*unpack(pieces.at[k])) for k in range(4)]
    whole = g[3].after(g[2]).after(g[1].after(g[0]))
    pack(total, whole.a, whole.cov + whole.cov.T, whole.b)
    take_half(half, total, place[3])


def members_before(pieces, place, which, direct, passed, ea, ez, eb):
    lay_out(pieces, place, which, direct, passed)
    me = place[which]
    ea[...], ez[...], eb[...] = neutral()

    def one(k, _):
        step = Step(*unpack(pieces.at[k])).after(Step(ea[...], ez[...], eb[...]))
        ea[...], ez[...], eb[...] = step.a, step.cov, step.b
        return 0

    lax.fori_loop(0, me, one, 0)


def before_y_kernel(place, direct, passed, later, ea, ez, eb, pieces):
    members_before(pieces, place, 2, direct, passed, ea, ez, eb)


def entry_kernel(place, direct, passed, ya, yz, yb, core, ea, ez, eb, pieces):
    members_before(pieces, place, 1, direct, passed, ea, ez, eb)
    c = place[3]
    last = Step(*[jnp.where(c == 1, u, v) for u, v in zip(unpack(core), neutral())])
    both = last.after(Step(ya[...], yz[...], yb[...])).after(Step(ea[...], ez[...], eb[...]))
    ea[...], ez[...], eb[...] = both.a, both.cov, both.b


def lane(x, i):
    return jnp.broadcast_to(x[:, i : i + 1], x.shape)


def factor_block(rows, o):
    tiles, count = len(rows), len(rows[0])
    for q in range(0, count, PB):
        a = {(t, s): lane(rows[0][q + t], o + q + s) for t in range(PB) for s in range(t, PB)}
        for t in range(PB):
            inv = lax.rsqrt(a[t, t])
            u = {s: a[t, s] * inv for s in range(t + 1, PB)}
            for s in range(t + 1, PB):
                for r in range(s, PB):
                    a[s, r] = a[s, r] - u[s] * u[r]
            for w in range(tiles):
                rows[w][q + t] = rows[w][q + t] * inv
                for s in range(t + 1, PB):
                    rows[w][q + s] = rows[w][q + s] - u[s] * rows[w][q + t]
        for i in range(q + PB, count):
            for t in range(PB):
                c = lane(rows[0][q + t], o + i)
                for w in range(tiles):
                    rows[w][i] = rows[w][i] - c * rows[w][q + t]


def strided(j, count, m):
    return pl.ds(STEPS * j + m, count, stride=STEPS)


def cholesky(cov, l_ref, logs_ref, u0, u1):
    us = (u0, u1)
    for j0 in range(0, N, NB):
        first, r0 = j0 // H, j0 + NB
        tiles = range(first, 2)
        for m in range(STEPS):
            for w in tiles:
                us[w][strided(j0, NB, m), :] = cov[m, j0:r0, H * w : H * w + H]
        rows = [[us[w][pl.ds(8 * (j0 + i), 8), :] for i in range(NB)] for w in tiles]
        factor_block(rows, j0 % H)
        for w in tiles:
            for i in range(NB):
                us[w][pl.ds(8 * (j0 + i), 8), :] = rows[w - first][i]
        if r0 == N:
            break
        for m in range(STEPS):
            u = jnp.concatenate([us[w][strided(j0, NB, m), :] for w in tiles], axis=1)
            left, right = split(u.T[r0 - H * first :, :]), split(u)
            cov[m, r0:, H * first :] = cov[m, r0:, H * first :] - mm3(left, right)
    r, c = grid_iota()
    diagonals = []
    for m in range(STEPS):
        a1 = u0[strided(0, H, m), :]
        a2 = u1[strided(H, H, m), :]
        diagonals += [jnp.sum(jnp.where(r == c, u, 0.0), axis=0, keepdims=True) for u in (a1, a2)]
        l_ref[m, 0:H, 0:H] = jnp.where(r <= c, a1, 0.0).T
        l_ref[m, H:, 0:H] = u1[strided(0, H, m), :].T
        l_ref[m, H:, H:] = jnp.where(r <= c, a2, 0.0).T
        l_ref[m, 0:H, H:] = jnp.zeros((H, H), f32)
    logs = jnp.sum(jnp.log(jnp.concatenate(diagonals, axis=0)), axis=0, keepdims=True)
    logs_ref[...] = jnp.broadcast_to(jnp.sum(logs, axis=1, keepdims=True), (1, H))


def final_kernel(place, direct, passed, ea, ez, eb, a_ref, p_ref, b_ref, m0_ref, l0_ref,
                 means, l_ref, logs, pieces, zs, ms, cov, u0, u1):
    lay_out(pieces, place, 0, direct, passed)
    l0 = split(l0_ref[...])
    zs[...] = 0.5 * mm3(l0, l0, 1, 1)
    ms[...] = jnp.broadcast_to(m0_ref[...], (8, N))

    def slab(k, _):
        zs[...], ms[...] = apply_to(Step(*unpack(pieces.at[k])), (zs[...], ms[...]))
        return 0

    lax.fori_loop(0, place[0], slab, 0)
    z, mean = apply_to(Step(ea[...], ez[...], eb[...]), (zs[...], ms[...]))
    state = split(z + z.T)
    for k in range(STEPS):
        spread, moved = through(split(a_ref[k]), state, mean)
        cov[k] = spread + p_ref[k]
        means[k : k + 1, :] = (moved + b_ref[k])[0:1, :]
    cholesky(cov, l_ref, logs, u0, u1)


VMEM = pl.BlockSpec(memory_space=pltpu.VMEM)
ANY = pl.BlockSpec(memory_space=pl.ANY)
HBM = pl.BlockSpec(memory_space=pltpu.HBM)
SMEM = pl.BlockSpec(memory_space=pltpu.SMEM)


def shape(*dims):
    return jax.ShapeDtypeStruct(dims, f32)


def call(kernel, outs, specs, scratch, name, mib, products):
    return pl.pallas_call(
        kernel,
        out_shape=outs,
        in_specs=specs,
        out_specs=(VMEM,) * len(outs),
        scratch_shapes=scratch,
        compiler_params=pltpu.CompilerParams(vmem_limit_bytes=mib * 2**20),
        cost_estimate=pl.CostEstimate(
            flops=products * 6 * N**3, bytes_accessed=8 * N * N * products, transcendentals=0
        ),
        name=name,
    )


def ring(axis, back):
    stride, count = {"c": (1, 2), "y": (2, 4), "x": (8, 4), "z": (32, 4)}[axis]
    pairs = []
    for i in range(128):
        p = (i // stride) % count
        pairs.append((i, i + ((p + back) % count - p) * stride))
    return pairs


def send(x, axis, back):
    return lax.ppermute(x, AXES, ring(axis, back))


def gather_ring(half, axis, beside):
    got = [send(half, axis, back) for back in (1, 2, 3)]
    direct = call(stack_kernel, (shape(3, HALF, N),), [VMEM] * 3 + [ANY], [], "stack_" + axis, 8, 1)(
        *got, beside
    )[0]
    return direct, send(direct, "c", 1)


def on_device(transitions, noise_factor, forcing, initial_mean, initial_factor):
    place = jnp.stack([lax.axis_index(axis) for axis in AXES]).astype(jnp.int32)
    stack = shape(STEPS, N, N)
    packed, half = shape(ROWS, N), shape(HALF, N)
    element = (shape(N, N), shape(N, N), shape(8, N))
    steps_in = [HBM] * 3
    buffers = [
        pltpu.VMEM((STEPS, N, N), f32),
        pltpu.VMEM((STEPS, N, N), f32),
        pltpu.VMEM((STEPS, N), f32),
        pltpu.SemaphoreType.DMA((STEPS, 2)),
        pltpu.SemaphoreType.DMA,
    ]
    lines = [pltpu.VMEM((4, ROWS, N), f32)]
    own = call(local_kernel, (packed,), steps_in, buffers, "local", 52, 29)(
        transitions, noise_factor, forcing
    )[0]
    other = send(own, "c", 1)
    mine, total = call(core_kernel, (half, packed), [SMEM, VMEM, VMEM], [], "core", 16, 3)(
        place, own, other
    )
    a, p, b = call(
        prefix_kernel, (stack, stack, shape(STEPS, 8, N)), steps_in + [ANY], buffers, "prefix", 52, 47
    )(transitions, noise_factor, forcing, total)

    def ring_total(which, axis, got):
        return call(
            lambda *refs: ring_kernel(which, *refs),
            (half, packed),
            [SMEM] + [VMEM] * 3,
            lines,
            "ring_" + axis,
            24,
            9,
        )(place, total, *got)

    along_y = gather_ring(mine, "y", b)
    mine, total = ring_total(2, "y", along_y)
    by_y = call(before_y_kernel, element, [SMEM, VMEM, VMEM, ANY], lines, "before_y", 24, 9)(
        place, *along_y, total
    )
    along_x = gather_ring(mine, "x", by_y[2])
    mine, total = ring_total(1, "x", along_x)
    entry = call(entry_kernel, element, [SMEM] + [VMEM] * 6, lines, "entry", 24, 15)(
        place, *along_x, *by_y, other
    )
    means, factors, logs = call(
        final_kernel,
        (shape(STEPS, N), stack, shape(1, H)),
        [SMEM] + [VMEM] * 10,
        [
            pltpu.VMEM((4, ROWS, N), f32),
            pltpu.VMEM((N, N), f32),
            pltpu.VMEM((8, N), f32),
            pltpu.VMEM((STEPS, N, N), f32),
            pltpu.VMEM((STEPS * N, H), f32),
            pltpu.VMEM((STEPS * N, H), f32),
        ],
        "final",
        48,
        32,
    )(place, *gather_ring(mine, "z", entry[2]), *entry, a, p, b, initial_mean[None], initial_factor)
    logs = lax.all_to_all(logs.reshape(H), AXES, 0, 0, tiled=True)
    log_scale = jnp.sum(logs) / (128 * STEPS * N)
    return means, factors, log_scale


def solution(mesh):
    cube = Mesh(mesh.devices.reshape(4, 4, 4, 2), AXES)
    return jax.shard_map(
        on_device,
        mesh=cube,
        in_specs=(P(AXES, None, None), P(AXES, None, None), P(AXES, None), P(), P()),
        out_specs=(P(AXES, None), P(AXES, None, None), P()),
        check_vma=False,
    )
```

```python
import functools

import jax
import jax.numpy as jnp
from jax import lax
from jax.experimental import pallas as pl
from jax.experimental.pallas import tpu as pltpu
from jax.sharding import Mesh, PartitionSpec as P

f32, bf16 = jnp.float32, jnp.bfloat16
AXES = ("z", "x", "y", "c")
N = 256
H = 128
STEPS = 8
HELD = STEPS // 2
ROWS = 400
HALF = ROWS // 2
PB = 8
NB = 32


def split(x):
    hi = x.astype(bf16)
    return hi, (x - hi.astype(f32)).astype(bf16)


def dg(a, b, ca, cb):
    return lax.dot_general(a, b, (((ca,), (cb,)), ((), ())), preferred_element_type=f32)


def mm3(a, b, ca=1, cb=0):
    return dg(a[0], b[0], ca, cb) + (dg(a[0], b[1], ca, cb) + dg(a[1], b[0], ca, cb))


def mm4(a, b):
    return dg(a[0], b[0], 1, 0) + ((dg(a[0], b[1], 1, 0) + dg(a[1], b[0], 1, 0)) + dg(a[1], b[1], 1, 0))


def through(a, cov, b):
    high, low = split(mm3(a, cov))
    wide = jnp.concatenate([b, b], axis=0)
    v1 = wide.astype(bf16)
    rest = wide - v1.astype(f32)
    v2 = rest.astype(bf16)
    v3 = (rest - v2.astype(f32)).astype(bf16)
    by_high = dg(jnp.concatenate([high, low, v1, v2, v3], axis=0), a[0], 1, 1)
    by_low = dg(jnp.concatenate([high, v1, v2], axis=0), a[1], 1, 1)
    out = by_high[:N] + (by_high[N : 2 * N] + by_low[:N])
    vec = by_high[2 * N + 32 : 2 * N + 40] + by_low[N + 16 : N + 24]
    vec = vec + (by_high[2 * N + 16 : 2 * N + 24] + by_low[N : N + 8])
    return out, by_high[2 * N : 2 * N + 8] + vec


def grid_iota():
    return (
        lax.broadcasted_iota(jnp.int32, (H, H), 0),
        lax.broadcasted_iota(jnp.int32, (H, H), 1),
    )


def pack(out, a, p, b):
    r, c = grid_iota()
    out[0:N, :] = a
    out[N : N + H, 0:H] = p[H:, :H]
    out[N : N + H, H:] = jnp.where(r >= c, p[:H, :H], p[H:, H:])
    diag = jnp.sum(jnp.where(r == c, p[H:, H:], 0.0), axis=0, keepdims=True)
    row = lax.broadcasted_iota(jnp.int32, (8, N), 0)
    wide = jnp.concatenate([diag, diag], axis=1)
    out[N + H : N + H + 8, :] = jnp.where(row == 0, b, jnp.broadcast_to(wide, (8, N)))
    out[N + H + 8 :, :] = jnp.zeros((8, N), f32)


def unpack(ref):
    r, c = grid_iota()
    a = ref[0:N, :]
    x = ref[N : N + H, H:]
    tail = ref[N + H : N + H + 8, :]
    d2 = tail[1:2, :H]
    z11 = jnp.where(r > c, x, jnp.where(r == c, 0.5 * x, 0.0))
    z22 = jnp.where(r < c, x, jnp.where(r == c, 0.5 * jnp.broadcast_to(d2, (H, H)), 0.0))
    top = jnp.concatenate([z11, jnp.zeros((H, H), f32)], axis=1)
    low = jnp.concatenate([ref[N : N + H, :H], z22], axis=1)
    return a, jnp.concatenate([top, low], axis=0), jnp.broadcast_to(tail[0:1, :], (8, N))


class Step:
    def __init__(self, a, cov, b):
        self.a, self.cov, self.b = a, cov, b
        self.a2, self.cov2 = split(a), split(cov)

    def after(self, earlier):
        cov, b = through(self.a2, earlier.cov2, earlier.b)
        return Step(mm4(self.a2, earlier.a2), cov + self.cov, b + self.b)


def apply_to(step, state):
    z, m = through(step.a2, split(state[0]), state[1])
    return z + step.cov, m + step.b


def fetch(steps, t_hbm, n_hbm, f_hbm, t_buf, n_buf, f_buf, sems, f_sem):
    copies = {}
    pushes = pltpu.make_async_copy(f_hbm, f_buf, f_sem)
    pushes.start()
    for k in steps:
        pair = [
            pltpu.make_async_copy(n_hbm.at[k], n_buf.at[k], sems.at[k, 0]),
            pltpu.make_async_copy(t_hbm.at[k], t_buf.at[k], sems.at[k, 1]),
        ]
        for copy in pair:
            copy.start()
        copies[k] = pair

    pushes.wait()

    def one(k):
        for copy in copies[k]:
            copy.wait()
        noise = split(n_buf[k])
        push = jnp.broadcast_to(f_buf[k : k + 1, :], (8, N))
        return Step(t_buf[k], mm3(noise, noise, 1, 1), push)

    return one


def local_kernel(t_hbm, n_hbm, f_hbm, total, *buffers):
    one = fetch(range(STEPS), t_hbm, n_hbm, f_hbm, *buffers)
    pairs = []
    for k in range(0, STEPS, 2):
        earlier, later = one(k), one(k + 1)
        pairs.append(later.after(earlier))
    whole = pairs[3].after(pairs[2]).after(pairs[1].after(pairs[0]))
    pack(total, whole.a, whole.cov, whole.b)


def put_step(refs, k, step):
    refs[0][k], refs[1][k], refs[2][k] = step.a, step.cov, step.b


def front_kernel(t_hbm, n_hbm, f_hbm, later, a_out, p_out, b_out, *buffers):
    out = (a_out, p_out, b_out)
    one = fetch(range(HELD), t_hbm, n_hbm, f_hbm, *buffers)
    first, second = one(0), one(1)
    pair = second.after(first)
    put_step(out, 0, first)
    put_step(out, 1, pair)
    third, fourth = one(2), one(3)
    put_step(out, 2, third.after(pair))
    put_step(out, 3, fourth.after(third).after(pair))


def back_kernel(t_hbm, n_hbm, f_hbm, a_front, p_front, b_front, later, a_out, p_out, b_out, *buffers):
    out = (a_out, p_out, b_out)
    one = fetch(range(HELD, STEPS), t_hbm, n_hbm, f_hbm, *buffers)
    fifth, sixth = one(4), one(5)
    front = Step(a_front[HELD - 1], p_front[HELD - 1], b_front[HELD - 1])
    put_step(out, 0, fifth.after(front))
    six = sixth.after(fifth).after(front)
    put_step(out, 1, six)
    seventh, eighth = one(6), one(7)
    put_step(out, 2, seventh.after(six))
    put_step(out, 3, eighth.after(seventh).after(six))


def take_half(half, whole, c):
    half[...] = whole[pl.ds(pl.multiple_of(c * HALF, 8), HALF), :]


def core_kernel(place, own, other, half, total):
    c = place[3]
    mine, theirs = unpack(own), unpack(other)
    earlier = Step(*[jnp.where(c == 0, u, v) for u, v in zip(mine, theirs)])
    later = Step(*[jnp.where(c == 0, v, u) for u, v in zip(mine, theirs)])
    both = later.after(earlier)
    pack(total, both.a, both.cov + both.cov.T, both.b)
    take_half(half, total, c)


def stack_kernel(r1, r2, r3, *refs):
    out = refs[-1]
    for k, r in enumerate((r1, r2, r3)):
        out[k] = r[...]


def lay_out(pieces, place, which, direct, passed):
    me, c = place[which], place[3]
    here = pl.multiple_of(c * HALF, 8)
    there = pl.multiple_of((1 - c) * HALF, 8)
    for back in (1, 2, 3):
        spot = lax.rem(me + 4 - back, 4)
        pieces[spot, pl.ds(here, HALF), :] = direct[back - 1]
        pieces[spot, pl.ds(there, HALF), :] = passed[back - 1]


def neutral():
    rows = lax.broadcasted_iota(jnp.int32, (N, N), 0)
    columns = lax.broadcasted_iota(jnp.int32, (N, N), 1)
    eye = jnp.where(rows == columns, 1.0, 0.0)
    return eye, jnp.zeros((N, N), f32), jnp.zeros((8, N), f32)


def ring_kernel(which, place, own, direct, passed, half, total, pieces):
    pieces[place[which]] = own[...]
    lay_out(pieces, place, which, direct, passed)
    g = [Step(*unpack(pieces.at[k])) for k in range(4)]
    whole = g[3].after(g[2]).after(g[1].after(g[0]))
    pack(total, whole.a, whole.cov + whole.cov.T, whole.b)
    take_half(half, total, place[3])


def members_before(pieces, place, which, direct, passed, ea, ez, eb):
    lay_out(pieces, place, which, direct, passed)
    me = place[which]
    ea[...], ez[...], eb[...] = neutral()

    def one(k, _):
        step = Step(*unpack(pieces.at[k])).after(Step(ea[...], ez[...], eb[...]))
        ea[...], ez[...], eb[...] = step.a, step.cov, step.b
        return 0

    lax.fori_loop(0, me, one, 0)


def before_y_kernel(place, direct, passed, later, ea, ez, eb, pieces):
    members_before(pieces, place, 2, direct, passed, ea, ez, eb)


def entry_kernel(place, direct, passed, ya, yz, yb, core, ea, ez, eb, pieces):
    members_before(pieces, place, 1, direct, passed, ea, ez, eb)
    c = place[3]
    last = Step(*[jnp.where(c == 1, u, v) for u, v in zip(unpack(core), neutral())])
    both = last.after(Step(ya[...], yz[...], yb[...])).after(Step(ea[...], ez[...], eb[...]))
    ea[...], ez[...], eb[...] = both.a, both.cov, both.b


def lane(x, i):
    return jnp.broadcast_to(x[:, i : i + 1], x.shape)


def factor_block(rows, o, beside):
    tiles, count = len(rows), len(rows[0])
    share = -(-len(beside) // (count // PB))
    for q in range(0, count, PB):
        a = {(t, s): lane(rows[0][q + t], o + q + s) for t in range(PB) for s in range(t, PB)}
        for work in beside[q // PB * share : (q // PB + 1) * share]:
            work()
        for t in range(PB):
            inv = lax.rsqrt(a[t, t])
            u = {s: a[t, s] * inv for s in range(t + 1, PB)}
            for s in range(t + 1, PB):
                for r in range(s, PB):
                    a[s, r] = a[s, r] - u[s] * u[r]
            for w in range(tiles):
                rows[w][q + t] = rows[w][q + t] * inv
                for s in range(t + 1, PB):
                    rows[w][q + s] = rows[w][q + s] - u[s] * rows[w][q + t]
        for i in range(q + PB, count):
            for t in range(PB):
                c = lane(rows[0][q + t], o + i)
                for w in range(tiles):
                    rows[w][i] = rows[w][i] - c * rows[w][q + t]


def strided(j, count, m):
    return pl.ds(STEPS * j + m, count, stride=STEPS)


def cholesky(cov, l_ref, logs_ref, u0, u1):
    us = (u0, u1)
    r, c = grid_iota()
    diagonals = []

    def put_left(m):
        top = u0[strided(0, H, m), :]
        diagonals.append(jnp.sum(jnp.where(r == c, top, 0.0), axis=0, keepdims=True))
        l_ref[m, 0:H, 0:H] = jnp.where(r <= c, top, 0.0).T
        l_ref[m, H:, 0:H] = u1[strided(0, H, m), :].T
        l_ref[m, 0:H, H:] = jnp.zeros((H, H), f32)

    def later_rows(m, j, first, left, right):
        cov[m, j:, H * first :] = cov[m, j:, H * first :] - mm3(left, right)

    for m in range(STEPS):
        for w in range(2):
            us[w][strided(0, NB, m), :] = cov[m, 0:NB, H * w : H * w + H]
    beside, outputs = [], []
    for j0 in range(0, N, NB):
        first, r0 = j0 // H, j0 + NB
        tiles = range(first, 2)
        if j0 == H:
            outputs = [functools.partial(put_left, m) for m in range(STEPS)]
        share = len(outputs) // max(1, (N - j0) // NB) if j0 >= H else 0
        beside, outputs = beside + outputs[:share], outputs[share:]
        rows = [[us[w][pl.ds(8 * (j0 + i), 8), :] for i in range(NB)] for w in tiles]
        factor_block(rows, j0 % H, beside)
        beside = []
        for w in tiles:
            for i in range(NB):
                us[w][pl.ds(8 * (j0 + i), 8), :] = rows[w - first][i]
        if r0 == N:
            break
        for m in range(STEPS):
            u = jnp.concatenate([us[w][strided(j0, NB, m), :] for w in tiles], axis=1)
            left, right = split(u.T[r0 - H * first :, :]), split(u)
            near = cov[m, r0 : r0 + NB, H * first :] - mm3([x[:NB] for x in left], right)
            for w in range(r0 // H, 2):
                us[w][strided(r0, NB, m), :] = near[:, H * (w - first) : H * (w - first) + H]
            if r0 + NB < N:
                rest = [x[NB:] for x in left]
                beside.append(functools.partial(later_rows, m, r0 + NB, first, rest, right))
    for m in range(STEPS):
        low = u1[strided(H, H, m), :]
        diagonals.append(jnp.sum(jnp.where(r == c, low, 0.0), axis=0, keepdims=True))
        l_ref[m, H:, H:] = jnp.where(r <= c, low, 0.0).T
    logs = jnp.sum(jnp.log(jnp.concatenate(diagonals, axis=0)), axis=0, keepdims=True)
    logs_ref[...] = jnp.broadcast_to(jnp.sum(logs, axis=1, keepdims=True), (1, H))


def final_kernel(place, direct, passed, ea, ez, eb, a_front, p_front, b_front, a_back, p_back, b_back, m0_ref, l0_ref,
                 means, l_ref, logs, pieces, zs, ms, cov, u0, u1):
    lay_out(pieces, place, 0, direct, passed)
    l0 = split(l0_ref[...])
    zs[...] = 0.5 * mm3(l0, l0, 1, 1)
    ms[...] = jnp.broadcast_to(m0_ref[...], (8, N))

    def slab(k, _):
        zs[...], ms[...] = apply_to(Step(*unpack(pieces.at[k])), (zs[...], ms[...]))
        return 0

    lax.fori_loop(0, place[0], slab, 0)
    z, mean = apply_to(Step(ea[...], ez[...], eb[...]), (zs[...], ms[...]))
    state = split(z + z.T)
    for k in range(STEPS):
        a_ref, p_ref, b_ref = (a_front, p_front, b_front) if k < HELD else (a_back, p_back, b_back)
        spread, moved = through(split(a_ref[k % HELD]), state, mean)
        cov[k] = spread + p_ref[k % HELD]
        means[k : k + 1, :] = (moved + b_ref[k % HELD])[0:1, :]
    cholesky(cov, l_ref, logs, u0, u1)


VMEM = pl.BlockSpec(memory_space=pltpu.VMEM)
ANY = pl.BlockSpec(memory_space=pl.ANY)
HBM = pl.BlockSpec(memory_space=pltpu.HBM)
SMEM = pl.BlockSpec(memory_space=pltpu.SMEM)


def shape(*dims):
    return jax.ShapeDtypeStruct(dims, f32)


def call(kernel, outs, specs, scratch, name, mib, products):
    return pl.pallas_call(
        kernel,
        out_shape=outs,
        in_specs=specs,
        out_specs=(VMEM,) * len(outs),
        scratch_shapes=scratch,
        compiler_params=pltpu.CompilerParams(vmem_limit_bytes=mib * 2**20),
        cost_estimate=pl.CostEstimate(
            flops=products * 6 * N**3, bytes_accessed=8 * N * N * products, transcendentals=0
        ),
        name=name,
    )


def along(axis, back):
    stride, count = {"c": (1, 2), "y": (2, 4), "x": (8, 4), "z": (32, 4)}[axis]
    pairs = []
    for i in range(128):
        p = (i // stride) % count
        pairs.append((i, i + ((p + back) % count - p) * stride))
    return pairs


def send(x, axis, back):
    return lax.ppermute(x, AXES, along(axis, back))


def gather_ring(half, axis, *beside):
    got = [send(half, axis, back) for back in (1, 2, 3)]
    direct = call(stack_kernel, (shape(3, HALF, N),), [VMEM] * 3 + [ANY] * len(beside), [], "stack_" + axis, 8, 1)(
        *got, *beside
    )[0]
    return direct, send(direct, "c", 1)


def on_device(transitions, noise_factor, forcing, initial_mean, initial_factor):
    place = jnp.stack([lax.axis_index(axis) for axis in AXES]).astype(jnp.int32)
    stack = shape(STEPS, N, N)
    packed, half = shape(ROWS, N), shape(HALF, N)
    element = (shape(N, N), shape(N, N), shape(8, N))
    steps_in = [HBM] * 3
    buffers = [
        pltpu.VMEM((STEPS, N, N), f32),
        pltpu.VMEM((STEPS, N, N), f32),
        pltpu.VMEM((STEPS, N), f32),
        pltpu.SemaphoreType.DMA((STEPS, 2)),
        pltpu.SemaphoreType.DMA,
    ]
    lines = [pltpu.VMEM((4, ROWS, N), f32)]
    own = call(local_kernel, (packed,), steps_in, buffers, "local", 52, 29)(
        transitions, noise_factor, forcing
    )[0]
    other = send(own, "c", 1)
    mine, total = call(core_kernel, (half, packed), [SMEM, VMEM, VMEM], [], "core", 16, 3)(
        place, own, other
    )
    held = (shape(HELD, N, N), shape(HELD, N, N), shape(HELD, 8, N))
    front = call(front_kernel, held, steps_in + [ANY], buffers, "front", 52, 22)(
        transitions, noise_factor, forcing, total
    )
    along_y = gather_ring(mine, "y", front[2])
    mine, total = call(
        lambda *refs: ring_kernel(2, *refs),
        (half, packed),
        [SMEM] + [VMEM] * 3,
        lines,
        "ring_y",
        24,
        9,
    )(place, total, *along_y)
    by_y = call(before_y_kernel, element, [SMEM, VMEM, VMEM, ANY], lines, "before_y", 24, 9)(
        place, *along_y, total
    )
    back = call(
        back_kernel, held, steps_in + [VMEM] * 3 + [ANY], buffers, "back", 52, 28
    )(transitions, noise_factor, forcing, *front, total)
    along_x = gather_ring(mine, "x", by_y[2], back[2])
    mine = call(
        lambda *refs: ring_kernel(1, *refs),
        (half,),
        [SMEM] + [VMEM] * 3,
        [pltpu.VMEM((ROWS, N), f32)] + lines,
        "ring_x",
        24,
        9,
    )(place, total, *along_x)[0]
    entry = call(entry_kernel, element, [SMEM] + [VMEM] * 6, lines, "entry", 24, 15)(
        place, *along_x, *by_y, other
    )
    means, factors, logs = call(
        final_kernel,
        (shape(STEPS, N), stack, shape(1, H)),
        [SMEM] + [VMEM] * 13,
        [
            pltpu.VMEM((4, ROWS, N), f32),
            pltpu.VMEM((N, N), f32),
            pltpu.VMEM((8, N), f32),
            pltpu.VMEM((STEPS, N, N), f32),
            pltpu.VMEM((STEPS * N, H), f32),
            pltpu.VMEM((STEPS * N, H), f32),
        ],
        "final",
        48,
        32,
    )(place, *gather_ring(mine, "z", entry[2]), *entry, *front, *back, initial_mean[None], initial_factor)
    logs = lax.all_to_all(logs.reshape(H), AXES, 0, 0, tiled=True)
    log_scale = jnp.sum(logs) / (128 * STEPS * N)
    return means, factors, log_scale


def solution(mesh):
    cube = Mesh(mesh.devices.reshape(4, 4, 4, 2), AXES)
    return jax.shard_map(
        on_device,
        mesh=cube,
        in_specs=(P(AXES, None, None), P(AXES, None, None), P(AXES, None), P(), P()),
        out_specs=(P(AXES, None), P(AXES, None, None), P()),
        check_vma=False,
    )
```

```python
import functools

import jax
import jax.numpy as jnp
from jax import lax
from jax.experimental import pallas as pl
from jax.experimental.pallas import tpu as pltpu
from jax.sharding import Mesh, PartitionSpec as P

f32, bf16 = jnp.float32, jnp.bfloat16
AXES = ("z", "x", "y", "c")
N = 256
H = 128
STEPS = 8
HELD = STEPS // 2
ROWS = 400
HALF = ROWS // 2
PB = 8
NB = 32


def split(x):
    hi = x.astype(bf16)
    return hi, (x - hi.astype(f32)).astype(bf16)


def dg(a, b, ca, cb):
    return lax.dot_general(a, b, (((ca,), (cb,)), ((), ())), preferred_element_type=f32)


def mm3(a, b, ca=1, cb=0):
    return dg(a[0], b[0], ca, cb) + (dg(a[0], b[1], ca, cb) + dg(a[1], b[0], ca, cb))


def mm4(a, b):
    return dg(a[0], b[0], 1, 0) + ((dg(a[0], b[1], 1, 0) + dg(a[1], b[0], 1, 0)) + dg(a[1], b[1], 1, 0))


def through(a, cov, b):
    high, low = split(mm3(a, cov))
    wide = jnp.concatenate([b, b], axis=0)
    v1 = wide.astype(bf16)
    rest = wide - v1.astype(f32)
    v2 = rest.astype(bf16)
    v3 = (rest - v2.astype(f32)).astype(bf16)
    by_high = dg(jnp.concatenate([high, low, v1, v2, v3], axis=0), a[0], 1, 1)
    by_low = dg(jnp.concatenate([high, v1, v2], axis=0), a[1], 1, 1)
    out = by_high[:N] + (by_high[N : 2 * N] + by_low[:N])
    vec = by_high[2 * N + 32 : 2 * N + 40] + by_low[N + 16 : N + 24]
    vec = vec + (by_high[2 * N + 16 : 2 * N + 24] + by_low[N : N + 8])
    return out, by_high[2 * N : 2 * N + 8] + vec


def grid_iota():
    return (
        lax.broadcasted_iota(jnp.int32, (H, H), 0),
        lax.broadcasted_iota(jnp.int32, (H, H), 1),
    )


def pack(out, a, p, b):
    r, c = grid_iota()
    out[0:N, :] = a
    out[N : N + H, 0:H] = p[H:, :H]
    out[N : N + H, H:] = jnp.where(r >= c, p[:H, :H], p[H:, H:])
    diag = jnp.sum(jnp.where(r == c, p[H:, H:], 0.0), axis=0, keepdims=True)
    row = lax.broadcasted_iota(jnp.int32, (8, N), 0)
    wide = jnp.concatenate([diag, diag], axis=1)
    out[N + H : N + H + 8, :] = jnp.where(row == 0, b, jnp.broadcast_to(wide, (8, N)))
    out[N + H + 8 :, :] = jnp.zeros((8, N), f32)


def unpack(ref):
    r, c = grid_iota()
    a = ref[0:N, :]
    x = ref[N : N + H, H:]
    tail = ref[N + H : N + H + 8, :]
    d2 = tail[1:2, :H]
    z11 = jnp.where(r > c, x, jnp.where(r == c, 0.5 * x, 0.0))
    z22 = jnp.where(r < c, x, jnp.where(r == c, 0.5 * jnp.broadcast_to(d2, (H, H)), 0.0))
    top = jnp.concatenate([z11, jnp.zeros((H, H), f32)], axis=1)
    low = jnp.concatenate([ref[N : N + H, :H], z22], axis=1)
    return a, jnp.concatenate([top, low], axis=0), jnp.broadcast_to(tail[0:1, :], (8, N))


class Step:
    def __init__(self, a, cov, b):
        self.a, self.cov, self.b = a, cov, b
        self.a2, self.cov2 = split(a), split(cov)

    def after(self, earlier):
        cov, b = through(self.a2, earlier.cov2, earlier.b)
        return Step(mm4(self.a2, earlier.a2), cov + self.cov, b + self.b)


def apply_to(step, state):
    z, m = through(step.a2, split(state[0]), state[1])
    return z + step.cov, m + step.b


def fetch(steps, t_hbm, n_hbm, f_hbm, t_buf, n_buf, f_buf, sems, f_sem):
    copies = {}
    pushes = pltpu.make_async_copy(f_hbm, f_buf, f_sem)
    pushes.start()
    for k in steps:
        pair = [
            pltpu.make_async_copy(n_hbm.at[k], n_buf.at[k], sems.at[k, 0]),
            pltpu.make_async_copy(t_hbm.at[k], t_buf.at[k], sems.at[k, 1]),
        ]
        for copy in pair:
            copy.start()
        copies[k] = pair

    pushes.wait()

    def one(k):
        for copy in copies[k]:
            copy.wait()
        noise = split(n_buf[k])
        push = jnp.broadcast_to(f_buf[k : k + 1, :], (8, N))
        return Step(t_buf[k], mm3(noise, noise, 1, 1), push)

    return one


def local_kernel(t_hbm, n_hbm, f_hbm, total, *buffers):
    one = fetch(range(STEPS), t_hbm, n_hbm, f_hbm, *buffers)
    pairs = []
    for k in range(0, STEPS, 2):
        earlier, later = one(k), one(k + 1)
        pairs.append(later.after(earlier))
    whole = pairs[3].after(pairs[2]).after(pairs[1].after(pairs[0]))
    pack(total, whole.a, whole.cov, whole.b)


def put_step(refs, k, step):
    refs[0][k], refs[1][k], refs[2][k] = step.a, step.cov, step.b


def front_kernel(t_hbm, n_hbm, f_hbm, later, a_out, p_out, b_out, *buffers):
    out = (a_out, p_out, b_out)
    one = fetch(range(HELD), t_hbm, n_hbm, f_hbm, *buffers)
    first, second = one(0), one(1)
    pair = second.after(first)
    put_step(out, 0, first)
    put_step(out, 1, pair)
    third, fourth = one(2), one(3)
    put_step(out, 2, third.after(pair))
    put_step(out, 3, fourth.after(third).after(pair))


def two_kernel(k, t_hbm, n_hbm, f_hbm, a_before, p_before, b_before, later, a_out, p_out, b_out, *buffers):
    out = (a_out, p_out, b_out)
    one = fetch(range(k, k + 2), t_hbm, n_hbm, f_hbm, *buffers)
    first, second = one(k), one(k + 1)
    last = a_before.shape[0] - 1
    before = Step(a_before[last], p_before[last], b_before[last])
    put_step(out, 0, first.after(before))
    put_step(out, 1, second.after(first).after(before))


def take_half(half, whole, c):
    half[...] = whole[pl.ds(pl.multiple_of(c * HALF, 8), HALF), :]


def core_kernel(place, own, other, half, total):
    c = place[3]
    mine, theirs = unpack(own), unpack(other)
    earlier = Step(*[jnp.where(c == 0, u, v) for u, v in zip(mine, theirs)])
    later = Step(*[jnp.where(c == 0, v, u) for u, v in zip(mine, theirs)])
    both = later.after(earlier)
    pack(total, both.a, both.cov + both.cov.T, both.b)
    take_half(half, total, c)


def pass_kernel(r, *refs):
    refs[-1][...] = r[...]


def lay_out(pieces, place, which, halves):
    me, c = place[which], place[3]
    here = pl.multiple_of(c * HALF, 8)
    there = pl.multiple_of((1 - c) * HALF, 8)
    for back in (1, 2, 3):
        spot = lax.rem(me + 4 - back, 4)
        pieces[spot, pl.ds(here, HALF), :] = halves[back - 1][...]
        pieces[spot, pl.ds(there, HALF), :] = halves[back + 2][...]


def neutral():
    rows = lax.broadcasted_iota(jnp.int32, (N, N), 0)
    columns = lax.broadcasted_iota(jnp.int32, (N, N), 1)
    eye = jnp.where(rows == columns, 1.0, 0.0)
    return eye, jnp.zeros((N, N), f32), jnp.zeros((8, N), f32)


def ring_kernel(which, place, own, halves, half, total, pieces):
    pieces[place[which]] = own[...]
    lay_out(pieces, place, which, halves)
    g = [Step(*unpack(pieces.at[k])) for k in range(4)]
    whole = g[3].after(g[2]).after(g[1].after(g[0]))
    pack(total, whole.a, whole.cov + whole.cov.T, whole.b)
    take_half(half, total, place[3])


def members_before(pieces, place, which, halves, ea, ez, eb):
    lay_out(pieces, place, which, halves)
    me = place[which]
    ea[...], ez[...], eb[...] = neutral()

    def one(k, _):
        step = Step(*unpack(pieces.at[k])).after(Step(ea[...], ez[...], eb[...]))
        ea[...], ez[...], eb[...] = step.a, step.cov, step.b
        return 0

    lax.fori_loop(0, me, one, 0)


def before_y_kernel(place, *refs):
    *halves, later, ea, ez, eb, pieces = refs
    members_before(pieces, place, 2, halves, ea, ez, eb)


def entry_kernel(place, *refs):
    *halves, ya, yz, yb, core, ea, ez, eb, pieces = refs
    members_before(pieces, place, 1, halves, ea, ez, eb)
    c = place[3]
    last = Step(*[jnp.where(c == 1, u, v) for u, v in zip(unpack(core), neutral())])
    both = last.after(Step(ya[...], yz[...], yb[...])).after(Step(ea[...], ez[...], eb[...]))
    ea[...], ez[...], eb[...] = both.a, both.cov, both.b


def lane(x, i):
    return jnp.broadcast_to(x[:, i : i + 1], x.shape)


def factor_block(rows, o, beside):
    tiles, count = len(rows), len(rows[0])
    share = -(-len(beside) // (count // PB))
    for q in range(0, count, PB):
        a = {(t, s): lane(rows[0][q + t], o + q + s) for t in range(PB) for s in range(t, PB)}
        for work in beside[q // PB * share : (q // PB + 1) * share]:
            work()
        for t in range(PB):
            inv = lax.rsqrt(a[t, t])
            u = {s: a[t, s] * inv for s in range(t + 1, PB)}
            for s in range(t + 1, PB):
                for r in range(s, PB):
                    a[s, r] = a[s, r] - u[s] * u[r]
            for w in range(tiles):
                rows[w][q + t] = rows[w][q + t] * inv
                for s in range(t + 1, PB):
                    rows[w][q + s] = rows[w][q + s] - u[s] * rows[w][q + t]
        for i in range(q + PB, count):
            for t in range(PB):
                c = lane(rows[0][q + t], o + i)
                for w in range(tiles):
                    rows[w][i] = rows[w][i] - c * rows[w][q + t]


def strided(j, count, m):
    return pl.ds(STEPS * j + m, count, stride=STEPS)


def cholesky(cov, l_ref, logs_ref, u0, u1):
    us = (u0, u1)
    r, c = grid_iota()
    diagonals = []

    def put_left(m):
        top = u0[strided(0, H, m), :]
        diagonals.append(jnp.sum(jnp.where(r == c, top, 0.0), axis=0, keepdims=True))
        l_ref[m, 0:H, 0:H] = jnp.where(r <= c, top, 0.0).T
        l_ref[m, H:, 0:H] = u1[strided(0, H, m), :].T
        l_ref[m, 0:H, H:] = jnp.zeros((H, H), f32)

    def later_rows(m, j, first, left, right):
        cov[m, j:, H * first :] = cov[m, j:, H * first :] - mm3(left, right)

    for m in range(STEPS):
        for w in range(2):
            us[w][strided(0, NB, m), :] = cov[m, 0:NB, H * w : H * w + H]
    beside, outputs = [], []
    for j0 in range(0, N, NB):
        first, r0 = j0 // H, j0 + NB
        tiles = range(first, 2)
        if j0 == H:
            outputs = [functools.partial(put_left, m) for m in range(STEPS)]
        share = len(outputs) // max(1, (N - j0) // NB) if j0 >= H else 0
        beside, outputs = beside + outputs[:share], outputs[share:]
        rows = [[us[w][pl.ds(8 * (j0 + i), 8), :] for i in range(NB)] for w in tiles]
        factor_block(rows, j0 % H, beside)
        beside = []
        for w in tiles:
            for i in range(NB):
                us[w][pl.ds(8 * (j0 + i), 8), :] = rows[w - first][i]
        if r0 == N:
            break
        for m in range(STEPS):
            u = jnp.concatenate([us[w][strided(j0, NB, m), :] for w in tiles], axis=1)
            left, right = split(u.T[r0 - H * first :, :]), split(u)
            near = cov[m, r0 : r0 + NB, H * first :] - mm3([x[:NB] for x in left], right)
            for w in range(r0 // H, 2):
                us[w][strided(r0, NB, m), :] = near[:, H * (w - first) : H * (w - first) + H]
            if r0 + NB < N:
                rest = [x[NB:] for x in left]
                beside.append(functools.partial(later_rows, m, r0 + NB, first, rest, right))
    for m in range(STEPS):
        low = u1[strided(H, H, m), :]
        diagonals.append(jnp.sum(jnp.where(r == c, low, 0.0), axis=0, keepdims=True))
        l_ref[m, H:, H:] = jnp.where(r <= c, low, 0.0).T
    logs = jnp.sum(jnp.log(jnp.concatenate(diagonals, axis=0)), axis=0, keepdims=True)
    logs_ref[...] = jnp.broadcast_to(jnp.sum(logs, axis=1, keepdims=True), (1, H))


def final_kernel(place, *refs):
    *steps, m0_ref, l0_ref, means, l_ref, logs, pieces, zs, ms, cov, u0, u1 = refs[9:]
    ea, ez, eb = refs[6:9]
    lay_out(pieces, place, 0, refs[:6])
    l0 = split(l0_ref[...])
    zs[...] = 0.5 * mm3(l0, l0, 1, 1)
    ms[...] = jnp.broadcast_to(m0_ref[...], (8, N))

    def slab(k, _):
        zs[...], ms[...] = apply_to(Step(*unpack(pieces.at[k])), (zs[...], ms[...]))
        return 0

    lax.fori_loop(0, place[0], slab, 0)
    z, mean = apply_to(Step(ea[...], ez[...], eb[...]), (zs[...], ms[...]))
    state = split(z + z.T)
    for k in range(STEPS):
        group, i = (0, k) if k < HELD else (3 * (1 + (k - HELD) // 2), (k - HELD) % 2)
        a_ref, p_ref, b_ref = steps[group : group + 3]
        spread, moved = through(split(a_ref[i]), state, mean)
        cov[k] = spread + p_ref[i]
        means[k : k + 1, :] = (moved + b_ref[i])[0:1, :]
    cholesky(cov, l_ref, logs, u0, u1)


VMEM = pl.BlockSpec(memory_space=pltpu.VMEM)
ANY = pl.BlockSpec(memory_space=pl.ANY)
HBM = pl.BlockSpec(memory_space=pltpu.HBM)
SMEM = pl.BlockSpec(memory_space=pltpu.SMEM)


def shape(*dims):
    return jax.ShapeDtypeStruct(dims, f32)


def call(kernel, outs, specs, scratch, name, mib, products):
    return pl.pallas_call(
        kernel,
        out_shape=outs,
        in_specs=specs,
        out_specs=(VMEM,) * len(outs),
        scratch_shapes=scratch,
        compiler_params=pltpu.CompilerParams(vmem_limit_bytes=mib * 2**20),
        cost_estimate=pl.CostEstimate(
            flops=products * 6 * N**3, bytes_accessed=8 * N * N * products, transcendentals=0
        ),
        name=name,
    )


def along(axis, back):
    stride, count = {"c": (1, 2), "y": (2, 4), "x": (8, 4), "z": (32, 4)}[axis]
    pairs = []
    for i in range(128):
        p = (i // stride) % count
        pairs.append((i, i + ((p + back) % count - p) * stride))
    return pairs


def send(x, axis, back):
    return lax.ppermute(x, AXES, along(axis, back))


def gather_ring(half, axis, *beside):
    got = [send(half, axis, back) for back in (1, 2, 3)]
    first = call(pass_kernel, (shape(HALF, N),), [VMEM] + [ANY] * len(beside), [], "pass_" + axis, 8, 1)(
        got[0], *beside
    )[0]
    return got + [send(r, "c", 1) for r in (first, got[1], got[2])]


def on_device(transitions, noise_factor, forcing, initial_mean, initial_factor):
    place = jnp.stack([lax.axis_index(axis) for axis in AXES]).astype(jnp.int32)
    stack = shape(STEPS, N, N)
    packed, half = shape(ROWS, N), shape(HALF, N)
    element = (shape(N, N), shape(N, N), shape(8, N))
    steps_in = [HBM] * 3
    buffers = [
        pltpu.VMEM((STEPS, N, N), f32),
        pltpu.VMEM((STEPS, N, N), f32),
        pltpu.VMEM((STEPS, N), f32),
        pltpu.SemaphoreType.DMA((STEPS, 2)),
        pltpu.SemaphoreType.DMA,
    ]
    lines = [pltpu.VMEM((4, ROWS, N), f32)]
    own = call(local_kernel, (packed,), steps_in, buffers, "local", 52, 29)(
        transitions, noise_factor, forcing
    )[0]
    other = send(own, "c", 1)
    mine, total = call(core_kernel, (half, packed), [SMEM, VMEM, VMEM], [], "core", 16, 3)(
        place, own, other
    )
    held = (shape(HELD, N, N), shape(HELD, N, N), shape(HELD, 8, N))
    front = call(front_kernel, held, steps_in + [ANY], buffers, "front", 52, 22)(
        transitions, noise_factor, forcing, total
    )
    two = (shape(2, N, N), shape(2, N, N), shape(2, 8, N))

    def next_two(k, before, later, name):
        return call(
            lambda *refs: two_kernel(k, *refs), two, steps_in + [VMEM] * 3 + [ANY], buffers, name, 52, 15
        )(transitions, noise_factor, forcing, *before, later)

    along_y = gather_ring(mine, "y", front[2])
    mine, total = call(
        lambda place, own, *refs: ring_kernel(2, place, own, refs[:6], *refs[6:]),
        (half, packed),
        [SMEM] + [VMEM] * 7,
        lines,
        "ring_y",
        24,
        9,
    )(place, total, *along_y)
    by_y = call(before_y_kernel, element, [SMEM] + [VMEM] * 6 + [ANY], lines, "before_y", 24, 9)(
        place, *along_y, total
    )
    third = next_two(HELD, front, total, "third")
    along_x = gather_ring(mine, "x", by_y[2], third[2])
    mine = call(
        lambda place, own, *refs: ring_kernel(
            1, place, own, refs[:6], refs[6], refs[7], refs[8]
        ),
        (half,),
        [SMEM] + [VMEM] * 7,
        [pltpu.VMEM((ROWS, N), f32)] + lines,
        "ring_x",
        24,
        9,
    )(place, total, *along_x)[0]
    entry = call(entry_kernel, element, [SMEM] + [VMEM] * 10, lines, "entry", 24, 15)(
        place, *along_x, *by_y, other
    )
    fourth = next_two(HELD + 2, third, mine, "fourth")
    means, factors, logs = call(
        final_kernel,
        (shape(STEPS, N), stack, shape(1, H)),
        [SMEM] + [VMEM] * 20,
        [
            pltpu.VMEM((4, ROWS, N), f32),
            pltpu.VMEM((N, N), f32),
            pltpu.VMEM((8, N), f32),
            pltpu.VMEM((STEPS, N, N), f32),
            pltpu.VMEM((STEPS * N, H), f32),
            pltpu.VMEM((STEPS * N, H), f32),
        ],
        "final",
        48,
        32,
    )(
        place,
        *gather_ring(mine, "z", entry[2], fourth[2]),
        *entry,
        *front,
        *third,
        *fourth,
        initial_mean[None],
        initial_factor,
    )
    logs = lax.all_to_all(logs.reshape(H), AXES, 0, 0, tiled=True)
    log_scale = jnp.sum(logs) / (128 * STEPS * N)
    return means, factors, log_scale


def solution(mesh):
    cube = Mesh(mesh.devices.reshape(4, 4, 4, 2), AXES)
    return jax.shard_map(
        on_device,
        mesh=cube,
        in_specs=(P(AXES, None, None), P(AXES, None, None), P(AXES, None), P(), P()),
        out_specs=(P(AXES, None), P(AXES, None, None), P()),
        check_vma=False,
    )
```

```python
import functools

import jax
import jax.numpy as jnp
from jax import lax
from jax.experimental import pallas as pl
from jax.experimental.pallas import tpu as pltpu
from jax.sharding import Mesh, PartitionSpec as P

f32, bf16 = jnp.float32, jnp.bfloat16
AXES = ("z", "x", "y", "c")
N = 256
H = 128
STEPS = 8
HELD = STEPS // 2
ROWS = 400
HALF = ROWS // 2
PB = 8
NB = 32


def split(x):
    hi = x.astype(bf16)
    return hi, (x - hi.astype(f32)).astype(bf16)


def dg(a, b, ca, cb):
    return lax.dot_general(a, b, (((ca,), (cb,)), ((), ())), preferred_element_type=f32)


def mm3(a, b, ca=1, cb=0):
    return dg(a[0], b[0], ca, cb) + (dg(a[0], b[1], ca, cb) + dg(a[1], b[0], ca, cb))


def mm4(a, b):
    return dg(a[0], b[0], 1, 0) + ((dg(a[0], b[1], 1, 0) + dg(a[1], b[0], 1, 0)) + dg(a[1], b[1], 1, 0))


def through(a, cov, b):
    high, low = split(mm3(a, cov))
    wide = jnp.concatenate([b, b], axis=0)
    v1 = wide.astype(bf16)
    rest = wide - v1.astype(f32)
    v2 = rest.astype(bf16)
    v3 = (rest - v2.astype(f32)).astype(bf16)
    by_high = dg(jnp.concatenate([high, low, v1, v2, v3], axis=0), a[0], 1, 1)
    by_low = dg(jnp.concatenate([high, v1, v2], axis=0), a[1], 1, 1)
    out = by_high[:N] + (by_high[N : 2 * N] + by_low[:N])
    vec = by_high[2 * N + 32 : 2 * N + 40] + by_low[N + 16 : N + 24]
    vec = vec + (by_high[2 * N + 16 : 2 * N + 24] + by_low[N : N + 8])
    return out, by_high[2 * N : 2 * N + 8] + vec


def grid_iota():
    return (
        lax.broadcasted_iota(jnp.int32, (H, H), 0),
        lax.broadcasted_iota(jnp.int32, (H, H), 1),
    )


def pack(out, a, p, b):
    r, c = grid_iota()
    out[0:N, :] = a
    out[N : N + H, 0:H] = p[H:, :H]
    out[N : N + H, H:] = jnp.where(r >= c, p[:H, :H], p[H:, H:])
    diag = jnp.sum(jnp.where(r == c, p[H:, H:], 0.0), axis=0, keepdims=True)
    row = lax.broadcasted_iota(jnp.int32, (8, N), 0)
    wide = jnp.concatenate([diag, diag], axis=1)
    out[N + H : N + H + 8, :] = jnp.where(row == 0, b, jnp.broadcast_to(wide, (8, N)))
    out[N + H + 8 :, :] = jnp.zeros((8, N), f32)


def unpack(ref):
    r, c = grid_iota()
    a = ref[0:N, :]
    x = ref[N : N + H, H:]
    tail = ref[N + H : N + H + 8, :]
    d2 = tail[1:2, :H]
    z11 = jnp.where(r > c, x, jnp.where(r == c, 0.5 * x, 0.0))
    z22 = jnp.where(r < c, x, jnp.where(r == c, 0.5 * jnp.broadcast_to(d2, (H, H)), 0.0))
    top = jnp.concatenate([z11, jnp.zeros((H, H), f32)], axis=1)
    low = jnp.concatenate([ref[N : N + H, :H], z22], axis=1)
    return a, jnp.concatenate([top, low], axis=0), jnp.broadcast_to(tail[0:1, :], (8, N))


class Step:
    def __init__(self, a, cov, b):
        self.a, self.cov, self.b = a, cov, b
        self.a2, self.cov2 = split(a), split(cov)

    def after(self, earlier):
        cov, b = through(self.a2, earlier.cov2, earlier.b)
        return Step(mm4(self.a2, earlier.a2), cov + self.cov, b + self.b)


def apply_to(step, state):
    z, m = through(step.a2, split(state[0]), state[1])
    return z + step.cov, m + step.b


def fetch(steps, t_hbm, n_hbm, f_hbm, t_buf, n_buf, f_buf, sems, f_sem):
    copies = {}
    pushes = pltpu.make_async_copy(f_hbm, f_buf, f_sem)
    pushes.start()
    for k in steps:
        pair = [
            pltpu.make_async_copy(n_hbm.at[k], n_buf.at[k], sems.at[k, 0]),
            pltpu.make_async_copy(t_hbm.at[k], t_buf.at[k], sems.at[k, 1]),
        ]
        for copy in pair:
            copy.start()
        copies[k] = pair

    pushes.wait()

    def one(k):
        for copy in copies[k]:
            copy.wait()
        noise = split(n_buf[k])
        push = jnp.broadcast_to(f_buf[k : k + 1, :], (8, N))
        return Step(t_buf[k], mm3(noise, noise, 1, 1), push)

    return one


def local_kernel(t_hbm, n_hbm, f_hbm, total, *buffers):
    one = fetch(range(STEPS), t_hbm, n_hbm, f_hbm, *buffers)
    pairs = []
    for k in range(0, STEPS, 2):
        earlier, later = one(k), one(k + 1)
        pairs.append(later.after(earlier))
    whole = pairs[3].after(pairs[2]).after(pairs[1].after(pairs[0]))
    pack(total, whole.a, whole.cov, whole.b)


def put_step(refs, k, step):
    refs[0][k], refs[1][k], refs[2][k] = step.a, step.cov, step.b


def front_kernel(t_hbm, n_hbm, f_hbm, later, a_out, p_out, b_out, *buffers):
    out = (a_out, p_out, b_out)
    one = fetch(range(HELD), t_hbm, n_hbm, f_hbm, *buffers)
    first, second = one(0), one(1)
    pair = second.after(first)
    put_step(out, 0, first)
    put_step(out, 1, pair)
    third, fourth = one(2), one(3)
    put_step(out, 2, third.after(pair))
    put_step(out, 3, fourth.after(third).after(pair))


def two_kernel(k, t_hbm, n_hbm, f_hbm, a_before, p_before, b_before, later, a_out, p_out, b_out, *buffers):
    out = (a_out, p_out, b_out)
    one = fetch(range(k, k + 2), t_hbm, n_hbm, f_hbm, *buffers)
    first, second = one(k), one(k + 1)
    last = a_before.shape[0] - 1
    before = Step(a_before[last], p_before[last], b_before[last])
    put_step(out, 0, first.after(before))
    put_step(out, 1, second.after(first).after(before))


def take_half(half, whole, c):
    half[...] = whole[pl.ds(pl.multiple_of(c * HALF, 8), HALF), :]


def core_kernel(place, own, other, half, total):
    c = place[3]
    mine, theirs = unpack(own), unpack(other)
    earlier = Step(*[jnp.where(c == 0, u, v) for u, v in zip(mine, theirs)])
    later = Step(*[jnp.where(c == 0, v, u) for u, v in zip(mine, theirs)])
    both = later.after(earlier)
    pack(total, both.a, both.cov + both.cov.T, both.b)
    take_half(half, total, c)


def pass_kernel(r, *refs):
    refs[-1][...] = r[...]


def lay_out(pieces, place, which, halves):
    me, c = place[which], place[3]
    here = pl.multiple_of(c * HALF, 8)
    there = pl.multiple_of((1 - c) * HALF, 8)
    for back in (1, 2, 3):
        spot = lax.rem(me + 4 - back, 4)
        pieces[spot, pl.ds(here, HALF), :] = halves[back - 1][...]
        pieces[spot, pl.ds(there, HALF), :] = halves[back + 2][...]


def neutral():
    rows = lax.broadcasted_iota(jnp.int32, (N, N), 0)
    columns = lax.broadcasted_iota(jnp.int32, (N, N), 1)
    eye = jnp.where(rows == columns, 1.0, 0.0)
    return eye, jnp.zeros((N, N), f32), jnp.zeros((8, N), f32)


def ring_kernel(which, place, own, halves, half, total, pieces):
    pieces[place[which]] = own[...]
    lay_out(pieces, place, which, halves)
    g = [Step(*unpack(pieces.at[k])) for k in range(4)]
    whole = g[3].after(g[2]).after(g[1].after(g[0]))
    pack(total, whole.a, whole.cov + whole.cov.T, whole.b)
    take_half(half, total, place[3])


def members_before(pieces, place, which, halves, ea, ez, eb):
    lay_out(pieces, place, which, halves)
    me = place[which]
    ea[...], ez[...], eb[...] = neutral()

    def one(k, _):
        step = Step(*unpack(pieces.at[k])).after(Step(ea[...], ez[...], eb[...]))
        ea[...], ez[...], eb[...] = step.a, step.cov, step.b
        return 0

    lax.fori_loop(0, me, one, 0)


def before_y_kernel(place, *refs):
    *halves, later, ea, ez, eb, pieces = refs
    members_before(pieces, place, 2, halves, ea, ez, eb)


def entry_kernel(place, *refs):
    *halves, ya, yz, yb, core, ea, ez, eb, pieces = refs
    members_before(pieces, place, 1, halves, ea, ez, eb)
    c = place[3]
    last = Step(*[jnp.where(c == 1, u, v) for u, v in zip(unpack(core), neutral())])
    both = last.after(Step(ya[...], yz[...], yb[...])).after(Step(ea[...], ez[...], eb[...]))
    ea[...], ez[...], eb[...] = both.a, both.cov, both.b


def lane(x, i):
    return jnp.broadcast_to(x[:, i : i + 1], x.shape)


def factor_block(rows, o, beside):
    tiles, count = len(rows), len(rows[0])
    share = -(-len(beside) // (count // PB))
    for q in range(0, count, PB):
        a = {(t, s): lane(rows[0][q + t], o + q + s) for t in range(PB) for s in range(t, PB)}
        for work in beside[q // PB * share : (q // PB + 1) * share]:
            work()
        for t in range(PB):
            inv = lax.rsqrt(a[t, t])
            u = {s: a[t, s] * inv for s in range(t + 1, PB)}
            for s in range(t + 1, PB):
                for r in range(s, PB):
                    a[s, r] = a[s, r] - u[s] * u[r]
            for w in range(tiles):
                rows[w][q + t] = rows[w][q + t] * inv
                for s in range(t + 1, PB):
                    rows[w][q + s] = rows[w][q + s] - u[s] * rows[w][q + t]
        for i in range(q + PB, count):
            for t in range(PB):
                c = lane(rows[0][q + t], o + i)
                for w in range(tiles):
                    rows[w][i] = rows[w][i] - c * rows[w][q + t]


def strided(j, count, m):
    return pl.ds(STEPS * j + m, count, stride=STEPS)


def cholesky(cov, l_ref, logs_ref, u0, u1):
    us = (u0, u1)
    r, c = grid_iota()
    diagonals = []

    def put_left(m):
        top = u0[strided(0, H, m), :]
        diagonals.append(jnp.sum(jnp.where(r == c, top, 0.0), axis=0, keepdims=True))
        l_ref[m, 0:H, 0:H] = jnp.where(r <= c, top, 0.0).T
        l_ref[m, H:, 0:H] = u1[strided(0, H, m), :].T
        l_ref[m, 0:H, H:] = jnp.zeros((H, H), f32)

    def later_rows(m, j, first, left, right):
        cov[m, j:, H * first :] = cov[m, j:, H * first :] - mm3(left, right)

    for m in range(STEPS):
        for w in range(2):
            us[w][strided(0, NB, m), :] = cov[m, 0:NB, H * w : H * w + H]
    beside, outputs = [], []
    for j0 in range(0, N, NB):
        first, r0 = j0 // H, j0 + NB
        tiles = range(first, 2)
        if j0 == H:
            outputs = [functools.partial(put_left, m) for m in range(STEPS)]
        share = len(outputs) // max(1, (N - j0) // NB) if j0 >= H else 0
        beside, outputs = beside + outputs[:share], outputs[share:]
        rows = [[us[w][pl.ds(8 * (j0 + i), 8), :] for i in range(NB)] for w in tiles]
        factor_block(rows, j0 % H, beside)
        beside = []
        for w in tiles:
            for i in range(NB):
                us[w][pl.ds(8 * (j0 + i), 8), :] = rows[w - first][i]
        if r0 == N:
            break
        for m in range(STEPS):
            u = jnp.concatenate([us[w][strided(j0, NB, m), :] for w in tiles], axis=1)
            left, right = split(u.T[r0 - H * first :, :]), split(u)
            near = cov[m, r0 : r0 + NB, H * first :] - mm3([x[:NB] for x in left], right)
            for w in range(r0 // H, 2):
                us[w][strided(r0, NB, m), :] = near[:, H * (w - first) : H * (w - first) + H]
            if r0 + NB < N:
                rest = [x[NB:] for x in left]
                beside.append(functools.partial(later_rows, m, r0 + NB, first, rest, right))
    for m in range(STEPS):
        low = u1[strided(H, H, m), :]
        diagonals.append(jnp.sum(jnp.where(r == c, low, 0.0), axis=0, keepdims=True))
        l_ref[m, H:, H:] = jnp.where(r <= c, low, 0.0).T
    logs = jnp.sum(jnp.log(jnp.concatenate(diagonals, axis=0)), axis=0, keepdims=True)
    logs_ref[...] = jnp.broadcast_to(jnp.sum(logs, axis=1, keepdims=True), (1, H))


def final_kernel(place, *refs):
    *steps, m0_ref, l0_ref, means, l_ref, logs, pieces, zs, ms, cov, u0, u1 = refs[9:]
    ea, ez, eb = refs[6:9]
    lay_out(pieces, place, 0, refs[:6])
    l0 = split(l0_ref[...])
    zs[...] = 0.5 * mm3(l0, l0, 1, 1)
    ms[...] = jnp.broadcast_to(m0_ref[...], (8, N))

    def slab(k, _):
        zs[...], ms[...] = apply_to(Step(*unpack(pieces.at[k])), (zs[...], ms[...]))
        return 0

    lax.fori_loop(0, place[0], slab, 0)
    z, mean = apply_to(Step(ea[...], ez[...], eb[...]), (zs[...], ms[...]))
    state = split(z + z.T)
    for k in range(STEPS):
        group, i = (0, k) if k < HELD else (3 * (1 + (k - HELD) // 2), (k - HELD) % 2)
        a_ref, p_ref, b_ref = steps[group : group + 3]
        spread, moved = through(split(a_ref[i]), state, mean)
        cov[k] = spread + p_ref[i]
        means[k : k + 1, :] = (moved + b_ref[i])[0:1, :]
    cholesky(cov, l_ref, logs, u0, u1)


VMEM = pl.BlockSpec(memory_space=pltpu.VMEM)
ANY = pl.BlockSpec(memory_space=pl.ANY)
HBM = pl.BlockSpec(memory_space=pltpu.HBM)
SMEM = pl.BlockSpec(memory_space=pltpu.SMEM)


def shape(*dims):
    return jax.ShapeDtypeStruct(dims, f32)


def call(kernel, outs, specs, scratch, name, mib, products):
    return pl.pallas_call(
        kernel,
        out_shape=outs,
        in_specs=specs,
        out_specs=(VMEM,) * len(outs),
        scratch_shapes=scratch,
        compiler_params=pltpu.CompilerParams(vmem_limit_bytes=mib * 2**20),
        cost_estimate=pl.CostEstimate(
            flops=products * 6 * N**3, bytes_accessed=8 * N * N * products, transcendentals=0
        ),
        name=name,
    )


def along(axis, back):
    stride, count = {"c": (1, 2), "y": (2, 4), "x": (8, 4), "z": (32, 4)}[axis]
    pairs = []
    for i in range(128):
        p = (i // stride) % count
        pairs.append((i, i + ((p + back) % count - p) * stride))
    return pairs


def send(x, axis, back):
    return lax.ppermute(x, AXES, along(axis, back))


def gather_ring(half, axis, *beside):
    got = [send(half, axis, back) for back in (1, 2, 3)]
    first = call(pass_kernel, (shape(HALF, N),), [VMEM] + [ANY] * len(beside), [], "pass_" + axis, 8, 1)(
        got[0], *beside
    )[0]
    return got + [send(r, "c", 1) for r in (first, got[1], got[2])]


def on_device(transitions, noise_factor, forcing, initial_mean, initial_factor):
    place = jnp.stack([lax.axis_index(axis) for axis in AXES]).astype(jnp.int32)
    stack = shape(STEPS, N, N)
    packed, half = shape(ROWS, N), shape(HALF, N)
    element = (shape(N, N), shape(N, N), shape(8, N))
    steps_in = [HBM] * 3
    buffers = [
        pltpu.VMEM((STEPS, N, N), f32),
        pltpu.VMEM((STEPS, N, N), f32),
        pltpu.VMEM((STEPS, N), f32),
        pltpu.SemaphoreType.DMA((STEPS, 2)),
        pltpu.SemaphoreType.DMA,
    ]
    lines = [pltpu.VMEM((4, ROWS, N), f32)]
    own = call(local_kernel, (packed,), steps_in, buffers, "local", 52, 29)(
        transitions, noise_factor, forcing
    )[0]
    other = send(own, "c", 1)
    mine, total = call(core_kernel, (half, packed), [SMEM, VMEM, VMEM], [], "core", 16, 3)(
        place, own, other
    )
    held = (shape(HELD, N, N), shape(HELD, N, N), shape(HELD, 8, N))
    front = call(front_kernel, held, steps_in + [ANY], buffers, "front", 52, 22)(
        transitions, noise_factor, forcing, total
    )
    two = (shape(2, N, N), shape(2, N, N), shape(2, 8, N))

    def next_two(k, before, later, name):
        return call(
            lambda *refs: two_kernel(k, *refs), two, steps_in + [VMEM] * 3 + [ANY], buffers, name, 52, 15
        )(transitions, noise_factor, forcing, *before, later)

    along_y = gather_ring(mine, "y", front[2])
    mine, total = call(
        lambda place, own, *refs: ring_kernel(2, place, own, refs[:6], *refs[6:]),
        (half, packed),
        [SMEM] + [VMEM] * 7,
        lines,
        "ring_y",
        24,
        9,
    )(place, total, *along_y)
    by_y = call(before_y_kernel, element, [SMEM] + [VMEM] * 6 + [ANY], lines, "before_y", 24, 9)(
        place, *along_y, total
    )
    third = next_two(HELD, front, total, "third")
    along_x = gather_ring(mine, "x", by_y[2], third[2])
    mine = call(
        lambda place, own, *refs: ring_kernel(
            1, place, own, refs[:6], refs[6], refs[7], refs[8]
        ),
        (half,),
        [SMEM] + [VMEM] * 7,
        [pltpu.VMEM((ROWS, N), f32)] + lines,
        "ring_x",
        24,
        9,
    )(place, total, *along_x)[0]
    entry = call(entry_kernel, element, [SMEM] + [VMEM] * 10, lines, "entry", 24, 15)(
        place, *along_x, *by_y, other
    )
    fourth = next_two(HELD + 2, third, mine, "fourth")
    means, factors, logs = call(
        final_kernel,
        (shape(STEPS, N), stack, shape(1, H)),
        [SMEM] + [VMEM] * 20,
        [
            pltpu.VMEM((4, ROWS, N), f32),
            pltpu.VMEM((N, N), f32),
            pltpu.VMEM((8, N), f32),
            pltpu.VMEM((STEPS, N, N), f32),
            pltpu.VMEM((STEPS * N, H), f32),
            pltpu.VMEM((STEPS * N, H), f32),
        ],
        "final",
        40,
        32,
    )(
        place,
        *gather_ring(mine, "z", entry[2], fourth[2]),
        *entry,
        *front,
        *third,
        *fourth,
        initial_mean[None],
        initial_factor,
    )
    logs = lax.all_to_all(logs.reshape(H), AXES, 0, 0, tiled=True)
    log_scale = jnp.sum(logs) / (128 * STEPS * N)
    return means, factors, log_scale


def solution(mesh):
    cube = Mesh(mesh.devices.reshape(4, 4, 4, 2), AXES)
    return jax.shard_map(
        on_device,
        mesh=cube,
        in_specs=(P(AXES, None, None), P(AXES, None, None), P(AXES, None), P(), P()),
        out_specs=(P(AXES, None), P(AXES, None, None), P()),
        check_vma=False,
    )
```
